32 devices in a mesh: outer: 4 (over x, core), inner: 8 (over z, y).
Axes of the slice: x: 2, y: 2, z: 4, core: 2. Of those that a mesh axis runs over, the one named last changes fastest.
Arguments:
- vertex: float32 [8192, 1024], P(('outer', 'inner')), may hold values from -1.5 to 1.5
- vertex_state: float32 [8192], P(('outer', 'inner')), may hold values from 0.05 to 0.5
- context: float32 [8192, 1024], P(('outer', 'inner')), may hold values from -1.5 to 1.5
- context_state: float32 [8192], P(('outer', 'inner')), may hold values from 0.05 to 0.5
- edge_source: int32 [32, 1536], P(('outer', 'inner')), may hold values from 0 to 255
- edge_target: int32 [32, 1536], P(('outer', 'inner')), may hold values from 0 to 255
Outputs:
- vertex_out: float32 [8192, 1024], P(('outer', 'inner'))
- vertex_state_out: float32 [8192], P(('outer', 'inner'))
- context_out: float32 [8192, 1024], P(('outer', 'inner'))
- context_state_out: float32 [8192], P(('outer', 'inner'))
The draws below stay inside these ranges and needn't reach their ends.
All inputs are finite; a program needn't handle non-finite values.
Results may differ from the reference program's by a relative error of at most 0.0019.
Values sent between devices are 32-bit elements; how exact they have to be, the bound alone decides.
A program may use at most 64 MiB of HBM per device.

```python
import math
import jax
import jax.numpy as jnp
from jax import lax

D = 1024
ROWS = 256
BLK = 256
EDGES = 512
ROUNDS = 3
BUCKETS = 32
N_OUTER = 4
N_INNER = 8


def plant(values, rng, least, top_value):
    extent = values.shape
    place = [jax.random.randint(jax.random.fold_in(rng, axis), (), 0, extent[axis]) for axis in range(len(extent))]
    values = values.at[tuple(place)].set(least)
    longest = extent.index(max(extent))
    place[longest] = (place[longest] + 1) % extent[longest]
    return values.at[tuple(place)].set(top_value)


def shard_levels(key, dims, cuts, smallest, largest):
    loudness = 1.0
    for dim, parts in cuts:
        heights = jax.random.uniform(jax.random.fold_in(jax.random.fold_in(key, 6), dim), (parts,), jnp.float32, smallest / len(cuts), largest / len(cuts))
        loudness = loudness * jnp.repeat(jnp.exp(heights), dims[dim] // parts).reshape((-1,) + (1,) * (len(dims) - 1 - dim))
    return loudness


def gaussian(key, dims, spread, bound, pieces=(), kind=jnp.bfloat16):
    array = jax.random.normal(key, dims, jnp.float32) * spread
    if len(pieces) > 0:
        array = shard_levels(key, dims, pieces, -0.22, 0.18) * array
    return jnp.clip(array, min=-bound, max=bound).astype(kind)


def setup_inputs(seed: int = 0) -> dict:
    splits = jax.random.split(jax.random.key(seed), 7)
    return {
        "vertex": gaussian(splits[0], (BUCKETS * ROWS, D), 0.25, 1.5, ((0, 32),), jnp.float32),
        "vertex_state": jnp.clip(jnp.exp(math.log(0.5) - 2.3025851 * jax.random.uniform(splits[1], (BUCKETS * ROWS,), jnp.float32) ** shard_levels(splits[1], (BUCKETS * ROWS,), ((0, 32),), -0.2, 0.2)), 0.05, 0.5),
        "context": gaussian(splits[2], (BUCKETS * BLK, D), 0.25, 1.5, ((0, 32),), jnp.float32),
        "context_state": jnp.clip(jnp.exp(math.log(0.5) - 2.3025851 * jax.random.uniform(splits[3], (BUCKETS * BLK,), jnp.float32) ** shard_levels(splits[3], (BUCKETS * BLK,), ((0, 32),), -0.2, 0.2)), 0.05, 0.5),
        "edge_source": plant(jax.random.randint(splits[4], (BUCKETS, ROUNDS * EDGES), 0, ROWS), jax.random.fold_in(splits[4], 1), 0, ROWS - 1).astype(jnp.int32),
        "edge_target": plant(jax.random.randint(splits[5], (BUCKETS, ROUNDS * EDGES), 0, BLK), jax.random.fold_in(splits[5], 1), 0, BLK - 1).astype(jnp.int32),
    }


def advance(items):
    rows, row_state, block, block_state, source, target = items
    rows_b = rows.astype(jnp.bfloat16)
    block_b = block.astype(jnp.bfloat16)
    scores = jnp.dot(rows_b, block_b.T, preferred_element_type=jnp.float32)
    prob = jax.nn.sigmoid(scores)
    source_hot = (source[:, None] == jnp.arange(ROWS, dtype=jnp.int32)[None, :]).astype(jnp.bfloat16)
    target_hot = (target[:, None] == jnp.arange(BLK, dtype=jnp.int32)[None, :]).astype(jnp.bfloat16)
    counts = jnp.dot(source_hot.T, target_hot, preferred_element_type=jnp.float32)
    grad = (prob / BLK - counts * (1.0 - prob)).astype(jnp.bfloat16)
    block_grad = jnp.dot(grad.T, rows_b, preferred_element_type=jnp.float32)
    rows_grad = jnp.dot(grad, block_b, preferred_element_type=jnp.float32)
    block_state = block_state + lax.optimization_barrier(jnp.mean(block_grad * block_grad, axis=1))
    block = block - 0.1 * block_grad / jnp.sqrt(block_state)[:, None]
    row_state = row_state + lax.optimization_barrier(jnp.mean(rows_grad * rows_grad, axis=1))
    rows = rows - 0.1 * rows_grad / jnp.sqrt(row_state)[:, None]
    return (rows, row_state, block, block_state)

def reference(vertex, vertex_state, context, context_state, edge_source, edge_target):
    buckets = N_OUTER * N_INNER
    rows = vertex.reshape(buckets, ROWS, D)
    row_state = vertex_state.reshape(buckets, ROWS)
    block = context.reshape(N_OUTER, N_INNER, BLK, D)
    block_state = context_state.reshape(N_OUTER, N_INNER, BLK)
    for step in range(ROUNDS):
        if step > 0:
            block = jnp.roll(block, 1, axis=1)
            block_state = jnp.roll(block_state, 1, axis=1)
        source = edge_source[:, step * EDGES:(step + 1) * EDGES]
        target = edge_target[:, step * EDGES:(step + 1) * EDGES]
        rows, row_state, flat_block, flat_state = lax.map(advance, (rows, row_state, block.reshape(buckets, BLK, D), block_state.reshape(buckets, BLK), source, target), batch_size=16)
        block = flat_block.reshape(N_OUTER, N_INNER, BLK, D)
        block_state = flat_state.reshape(N_OUTER, N_INNER, BLK)
    block = jnp.roll(block, 1, axis=0)
    block_state = jnp.roll(block_state, 1, axis=0)
    return (rows.reshape(buckets * ROWS, D), row_state.reshape(buckets * ROWS), block.reshape(buckets * BLK, D), block_state.reshape(buckets * BLK))
```

```python
import functools

import jax
import jax.numpy as jnp
from jax import lax
from jax.experimental import pallas as pl
from jax.experimental.pallas import tpu as pltpu
from jax.sharding import PartitionSpec as P

ROUNDS = 3
CHUNK = 32
DEPTH = 2

MESH = pl.DeviceIdType.MESH
BF16 = jnp.bfloat16
F32 = jnp.float32


def kernel(
    n_outer,
    n_inner,
    vertex,
    vertex_state,
    context,
    context_state,
    edge_source,
    edge_target,
    vertex_out,
    vertex_state_out,
    context_out,
    context_state_out,
    rows,
    rows_b,
    row_state,
    block,
    state,
    block_b,
    grads,
    counts,
    load_sem,
    send_sem,
    recv_sem,
    state_send_sem,
    state_recv_sem,
):
    pieces, chunk, width = context.shape
    row_count = rows.shape[0]
    block_rows = pieces * chunk
    edges = edge_source.shape[1] // ROUNDS
    hops = (ROUNDS - 1) * pieces

    i = lax.axis_index("inner")
    o = lax.axis_index("outer")
    right = {"inner": lax.rem(i + 1, n_inner)}
    left = {"inner": lax.rem(i + n_inner - 1, n_inner)}
    ahead = {"outer": lax.rem(o + 1, n_outer)}
    behind = {"outer": lax.rem(o + n_outer - 1, n_outer)}

    barrier = pltpu.get_barrier_semaphore()
    for neighbour in (left, right, behind, ahead):
        pl.semaphore_signal(barrier, inc=1, device_id=neighbour, device_id_type=MESH)

    load_rows = pltpu.make_async_copy(vertex, rows, load_sem.at[0])
    load_first = pltpu.make_async_copy(context.at[0], block.at[0], load_sem.at[1])
    load_rest = pltpu.make_async_copy(
        context.at[pl.ds(1, pieces - 1)], block.at[pl.ds(1, pieces - 1)], load_sem.at[2]
    )
    load_rows.start()
    load_first.start()
    load_rest.start()

    def hop(s):
        return pltpu.make_async_remote_copy(
            src_ref=block.at[s],
            dst_ref=block.at[s + pieces],
            send_sem=send_sem.at[s],
            recv_sem=recv_sem.at[s + pieces],
            device_id=right,
            device_id_type=MESH,
        )

    def state_hop(s):
        return pltpu.make_async_remote_copy(
            src_ref=state.at[s],
            dst_ref=state.at[s + pieces],
            send_sem=state_send_sem.at[s],
            recv_sem=state_recv_sem.at[s + pieces],
            device_id=right,
            device_id_type=MESH,
        )

    def leave(k):
        return pltpu.make_async_remote_copy(
            src_ref=block.at[hops + k],
            dst_ref=context_out.at[k],
            send_sem=send_sem.at[hops + k],
            recv_sem=recv_sem.at[hops + pieces + k],
            device_id=ahead,
            device_id_type=MESH,
        )

    def state_leave(k):
        return pltpu.make_async_remote_copy(
            src_ref=state.at[hops + k],
            dst_ref=state.at[hops + pieces + k],
            send_sem=state_send_sem.at[hops + k],
            recv_sem=state_recv_sem.at[hops + pieces + k],
            device_id=ahead,
            device_id_type=MESH,
        )

    def count(r):
        span = pl.ds(r * edges, edges)
        target_hot = (
            edge_target[:, span] == lax.broadcasted_iota(jnp.int32, (block_rows, edges), 0)
        ).astype(F32).astype(BF16)
        source_hot = (
            edge_source[:, span] == lax.broadcasted_iota(jnp.int32, (row_count, edges), 0)
        ).astype(F32).astype(BF16)
        counts[r] = lax.dot_general(
            target_hot, source_hot, (((1,), (1,)), ((), ())), preferred_element_type=F32
        ).reshape(pieces, chunk, row_count)

    def update_chunk(slot, r, k):
        held = block[slot]
        held_b = held.astype(BF16)
        block_b[k] = held_b
        scores = lax.dot_general(
            held_b, rows_b[...], (((1,), (1,)), ((), ())), preferred_element_type=F32
        )
        prob = 1.0 / (1.0 + jnp.exp(-scores))
        grad = (prob * (1.0 / block_rows) - counts[r, k] * (1.0 - prob)).astype(BF16)
        grads[k] = grad
        chunk_grad = jnp.dot(grad, rows_b[...], preferred_element_type=F32)
        place = lax.broadcasted_iota(jnp.int32, (chunk, block_rows), 0) + k * chunk
        lane = lax.broadcasted_iota(jnp.int32, (chunk, block_rows), 1)
        mine = place == lane
        total = jnp.sum(jnp.where(mine, state[slot], 0.0), axis=1, keepdims=True)
        total = total + jnp.sum(chunk_grad * chunk_grad, axis=1, keepdims=True) * (1.0 / width)
        block[slot] = held - chunk_grad * (0.1 * lax.rsqrt(total))
        state[slot] = jnp.sum(jnp.where(mine, total, 0.0), axis=0, keepdims=True)

    def update_rows():
        rows_grad = lax.dot_general(
            grads[...].reshape(block_rows, row_count),
            block_b[...].reshape(block_rows, width),
            (((0,), (0,)), ((), ())),
            preferred_element_type=F32,
        )
        total = row_state[...] + jnp.sum(rows_grad * rows_grad, axis=1, keepdims=True) * (
            1.0 / width
        )
        row_state[...] = total
        rows[...] = rows[...] - rows_grad * (0.1 * lax.rsqrt(total))
        rows_b[...] = rows[...].astype(BF16)

    eye = lax.broadcasted_iota(jnp.int32, (row_count, row_count), 0) == lax.broadcasted_iota(
        jnp.int32, (row_count, row_count), 1
    )
    row_state[...] = jnp.sum(jnp.where(eye, vertex_state[...], 0.0), axis=1, keepdims=True)
    for k in range(pieces):
        state[k] = context_state[...]
    count(0)
    load_rows.wait()
    rows_b[...] = rows[...].astype(BF16)
    load_first.wait()
    update_chunk(0, 0, 0)
    pl.semaphore_wait(barrier, 4)
    hop(0).start()
    state_hop(0).start()
    load_rest.wait()

    @pl.loop(1, pieces)
    def _(k):
        update_chunk(k, 0, k)

        @pl.when(k < DEPTH)
        def _():
            hop(k).start()
            state_hop(k).start()

    for r in range(1, ROUNDS):
        count(r)
    update_rows()

    for r in range(1, ROUNDS):

        @pl.loop(0, pieces)
        def _(k):
            s = (r - 1) * pieces + k
            hop(s).wait_send()
            state_hop(s).wait_send()

            @pl.when(s + DEPTH < hops)
            def _():
                hop(s + DEPTH).start()
                state_hop(s + DEPTH).start()

            hop(s).wait_recv()
            state_hop(s).wait_recv()
            update_chunk(s + pieces, r, k)
            if r == ROUNDS - 1:
                leave(k).start()
                state_leave(k).start()

        update_rows()

    store_rows = pltpu.make_async_copy(rows, vertex_out, load_sem.at[0])
    store_rows.start()
    vertex_state_out[...] = jnp.sum(jnp.where(eye, row_state[...], 0.0), axis=0, keepdims=True)

    @pl.loop(0, pieces)
    def _(k):
        leave(k).wait()
        state_leave(k).wait()

    context_state_out[...] = jnp.sum(state[pl.ds(hops + pieces, pieces)], axis=0)
    store_rows.wait()


def body(n_outer, n_inner, vertex, vertex_state, context, context_state, edge_source, edge_target):
    row_count, width = vertex.shape
    block_rows = context.shape[0]
    pieces = block_rows // CHUNK
    slots = ROUNDS * pieces
    whole = pl.BlockSpec(memory_space=pl.ANY)
    small = pl.BlockSpec(memory_space=pltpu.VMEM)
    vertex_out, vertex_state_out, context_out, context_state_out = pl.pallas_call(
        functools.partial(kernel, n_outer, n_inner),
        out_shape=(
            jax.ShapeDtypeStruct((row_count, width), F32),
            jax.ShapeDtypeStruct((1, row_count), F32),
            jax.ShapeDtypeStruct((pieces, CHUNK, width), F32),
            jax.ShapeDtypeStruct((1, block_rows), F32),
        ),
        in_specs=[whole, small, whole, small, small, small],
        out_specs=(whole, small, whole, small),
        scratch_shapes=[
            pltpu.VMEM((row_count, width), F32),
            pltpu.VMEM((row_count, width), BF16),
            pltpu.VMEM((row_count, 1), F32),
            pltpu.VMEM((slots, CHUNK, width), F32),
            pltpu.VMEM((slots + pieces, 1, block_rows), F32),
            pltpu.VMEM((pieces, CHUNK, width), BF16),
            pltpu.VMEM((pieces, CHUNK, row_count), BF16),
            pltpu.VMEM((ROUNDS, pieces, CHUNK, row_count), F32),
            pltpu.SemaphoreType.DMA((3,)),
            pltpu.SemaphoreType.DMA((slots,)),
            pltpu.SemaphoreType.DMA((slots + pieces,)),
            pltpu.SemaphoreType.DMA((slots,)),
            pltpu.SemaphoreType.DMA((slots + pieces,)),
        ],
        compiler_params=pltpu.CompilerParams(
            collective_id=0, has_side_effects=True, vmem_limit_bytes=32 * 1024 * 1024
        ),
        cost_estimate=pl.CostEstimate(
            flops=ROUNDS * 2 * row_count * block_rows * (3 * width + 512),
            bytes_accessed=16 * row_count * width,
            transcendentals=ROUNDS * row_count * block_rows,
        ),
    )(
        vertex,
        vertex_state.reshape(1, row_count),
        context.reshape(pieces, CHUNK, width),
        context_state.reshape(1, block_rows),
        edge_source,
        edge_target,
    )
    return (
        vertex_out,
        vertex_state_out.reshape(row_count),
        context_out.reshape(block_rows, width),
        context_state_out.reshape(block_rows),
    )


def solution(mesh):
    matrix = P(("outer", "inner"), None)
    vector = P(("outer", "inner"))
    return jax.shard_map(
        functools.partial(body, mesh.shape["outer"], mesh.shape["inner"]),
        mesh=mesh,
        in_specs=(matrix, vector, matrix, vector, matrix, matrix),
        out_specs=(matrix, vector, matrix, vector),
        check_vma=False,
    )
```

```python
import functools

import jax
import jax.numpy as jnp
from jax import lax
from jax.experimental import pallas as pl
from jax.experimental.pallas import tpu as pltpu
from jax.sharding import PartitionSpec as P

ROUNDS = 3
CHUNK = 32
DEPTH = 4

MESH = pl.DeviceIdType.MESH
BF16 = jnp.bfloat16
F32 = jnp.float32


def kernel(
    n_outer,
    n_inner,
    vertex,
    vertex_state_in,
    context,
    context_state_in,
    edge_source_in,
    edge_target_in,
    rows,
    vertex_state_out,
    context_out,
    context_state_out,
    vertex_state,
    context_state,
    edge_source,
    edge_target,
    rows_b,
    row_state,
    block,
    state,
    block_b,
    grads,
    counts,
    load_sem,
    send_sem,
    recv_sem,
    state_send_sem,
    state_recv_sem,
):
    pieces, chunk, width = context.shape
    row_count = rows.shape[0]
    block_rows = pieces * chunk
    edges = edge_source_in.shape[1] // ROUNDS
    hops = (ROUNDS - 1) * pieces

    i = lax.axis_index("inner")
    o = lax.axis_index("outer")
    right = {"inner": lax.rem(i + 1, n_inner)}
    left = {"inner": lax.rem(i + n_inner - 1, n_inner)}
    ahead = {"outer": lax.rem(o + 1, n_outer)}
    behind = {"outer": lax.rem(o + n_outer - 1, n_outer)}

    barrier = pltpu.get_barrier_semaphore()
    for neighbour in (left, right, behind, ahead):
        pl.semaphore_signal(barrier, inc=1, device_id=neighbour, device_id_type=MESH)

    small_loads = [
        pltpu.make_async_copy(source, target, load_sem.at[3 + n])
        for n, (source, target) in enumerate(
            (
                (edge_source_in, edge_source),
                (edge_target_in, edge_target),
                (vertex_state_in, vertex_state),
                (context_state_in, context_state),
            )
        )
    ]
    for load in small_loads:
        load.start()
    load_rows = pltpu.make_async_copy(vertex, rows, load_sem.at[0])
    load_first = pltpu.make_async_copy(context.at[0], block.at[0], load_sem.at[1])
    load_rest = pltpu.make_async_copy(
        context.at[pl.ds(1, pieces - 1)], block.at[pl.ds(1, pieces - 1)], load_sem.at[2]
    )
    load_rows.start()
    load_first.start()
    load_rest.start()

    def hop(s):
        return pltpu.make_async_remote_copy(
            src_ref=block.at[s],
            dst_ref=block.at[s + pieces],
            send_sem=send_sem.at[s],
            recv_sem=recv_sem.at[s + pieces],
            device_id=right,
            device_id_type=MESH,
        )

    def state_hop(s):
        return pltpu.make_async_remote_copy(
            src_ref=state.at[s],
            dst_ref=state.at[s + pieces],
            send_sem=state_send_sem.at[s],
            recv_sem=state_recv_sem.at[s + pieces],
            device_id=right,
            device_id_type=MESH,
        )

    def leave(k):
        return pltpu.make_async_remote_copy(
            src_ref=block.at[hops + k],
            dst_ref=context_out.at[k],
            send_sem=send_sem.at[hops + k],
            recv_sem=recv_sem.at[hops + pieces + k],
            device_id=ahead,
            device_id_type=MESH,
        )

    def state_leave(k):
        return pltpu.make_async_remote_copy(
            src_ref=state.at[hops + k],
            dst_ref=state.at[hops + pieces + k],
            send_sem=state_send_sem.at[hops + k],
            recv_sem=state_recv_sem.at[hops + pieces + k],
            device_id=ahead,
            device_id_type=MESH,
        )

    def count(r):
        span = pl.ds(r * edges, edges)
        target_hot = (
            edge_target[:, span] == lax.broadcasted_iota(jnp.int32, (block_rows, edges), 0)
        ).astype(F32).astype(BF16)
        source_hot = (
            edge_source[:, span] == lax.broadcasted_iota(jnp.int32, (row_count, edges), 0)
        ).astype(F32).astype(BF16)
        counts[r] = lax.dot_general(
            target_hot, source_hot, (((1,), (1,)), ((), ())), preferred_element_type=F32
        ).reshape(pieces, chunk, row_count)

    def update_chunk(slot, r, k):
        held = block[slot]
        held_b = held.astype(BF16)
        block_b[k] = held_b
        scores = lax.dot_general(
            held_b, rows_b[...], (((1,), (1,)), ((), ())), preferred_element_type=F32
        )
        prob = 1.0 / (1.0 + jnp.exp(-scores))
        grad = (prob * (1.0 / block_rows) - counts[r, k] * (1.0 - prob)).astype(BF16)
        grads[k] = grad
        chunk_grad = jnp.dot(grad, rows_b[...], preferred_element_type=F32)
        place = lax.broadcasted_iota(jnp.int32, (chunk, block_rows), 0) + k * chunk
        lane = lax.broadcasted_iota(jnp.int32, (chunk, block_rows), 1)
        mine = place == lane
        total = jnp.sum(jnp.where(mine, state[slot], 0.0), axis=1, keepdims=True)
        total = total + jnp.sum(chunk_grad * chunk_grad, axis=1, keepdims=True) * (1.0 / width)
        block[slot] = held - chunk_grad * (0.1 * lax.rsqrt(total))
        state[slot] = jnp.sum(jnp.where(mine, total, 0.0), axis=0, keepdims=True)

    def update_rows():
        rows_grad = lax.dot_general(
            grads[...].reshape(block_rows, row_count),
            block_b[...].reshape(block_rows, width),
            (((0,), (0,)), ((), ())),
            preferred_element_type=F32,
        )
        total = row_state[...] + jnp.sum(rows_grad * rows_grad, axis=1, keepdims=True) * (
            1.0 / width
        )
        row_state[...] = total
        rows[...] = rows[...] - rows_grad * (0.1 * lax.rsqrt(total))
        rows_b[...] = rows[...].astype(BF16)

    for load in small_loads:
        load.wait()
    eye = lax.broadcasted_iota(jnp.int32, (row_count, row_count), 0) == lax.broadcasted_iota(
        jnp.int32, (row_count, row_count), 1
    )
    row_state[...] = jnp.sum(jnp.where(eye, vertex_state[...], 0.0), axis=1, keepdims=True)
    for k in range(pieces):
        state[k] = context_state[...]
    count(0)
    load_rows.wait()
    rows_b[...] = rows[...].astype(BF16)
    load_first.wait()
    update_chunk(0, 0, 0)
    pl.semaphore_wait(barrier, 4)
    hop(0).start()
    state_hop(0).start()
    load_rest.wait()

    @pl.loop(1, pieces)
    def _(k):
        update_chunk(k, 0, k)

        @pl.when(k < DEPTH)
        def _():
            hop(k).start()
            state_hop(k).start()

    for r in range(1, ROUNDS):
        count(r)
    update_rows()

    for r in range(1, ROUNDS):

        @pl.loop(0, pieces)
        def _(k):
            s = (r - 1) * pieces + k
            hop(s).wait_send()
            state_hop(s).wait_send()

            @pl.when(s + DEPTH < hops)
            def _():
                hop(s + DEPTH).start()
                state_hop(s + DEPTH).start()

            hop(s).wait_recv()
            state_hop(s).wait_recv()
            update_chunk(s + pieces, r, k)
            if r == ROUNDS - 1:
                leave(k).start()
                state_leave(k).start()

        update_rows()

    vertex_state_out[...] = jnp.sum(jnp.where(eye, row_state[...], 0.0), axis=0, keepdims=True)

    @pl.loop(0, pieces)
    def _(k):
        leave(k).wait()
        state_leave(k).wait()

    context_state_out[...] = jnp.sum(state[pl.ds(hops + pieces, pieces)], axis=0)


def store_kernel(*refs):
    sources, targets, sems = refs[:4], refs[4:8], refs[8]
    copies = [
        pltpu.make_async_copy(source, target, sems.at[n])
        for n, (source, target) in enumerate(zip(sources, targets))
    ]
    for copy in copies:
        copy.start()
    for copy in copies:
        copy.wait()


def body(n_outer, n_inner, vertex, vertex_state, context, context_state, edge_source, edge_target):
    row_count, width = vertex.shape
    block_rows = context.shape[0]
    pieces = block_rows // CHUNK
    slots = ROUNDS * pieces
    far = pl.BlockSpec(memory_space=pltpu.HBM)
    near = pl.BlockSpec(memory_space=pltpu.VMEM)
    shapes = (
        (row_count, width),
        (1, row_count),
        (pieces, CHUNK, width),
        (1, block_rows),
    )
    results = pl.pallas_call(
        functools.partial(kernel, n_outer, n_inner),
        out_shape=tuple(pltpu.VMEM(shape, F32) for shape in shapes),
        in_specs=[far] * 6,
        out_specs=(near,) * 4,
        scratch_shapes=[
            pltpu.VMEM((1, row_count), F32),
            pltpu.VMEM((1, block_rows), F32),
            pltpu.VMEM(edge_source.shape, jnp.int32),
            pltpu.VMEM(edge_target.shape, jnp.int32),
            pltpu.VMEM((row_count, width), BF16),
            pltpu.VMEM((row_count, 1), F32),
            pltpu.VMEM((slots, CHUNK, width), F32),
            pltpu.VMEM((slots + pieces, 1, block_rows), F32),
            pltpu.VMEM((pieces, CHUNK, width), BF16),
            pltpu.VMEM((pieces, CHUNK, row_count), BF16),
            pltpu.VMEM((ROUNDS, pieces, CHUNK, row_count), F32),
            pltpu.SemaphoreType.DMA((7,)),
            pltpu.SemaphoreType.DMA((slots,)),
            pltpu.SemaphoreType.DMA((slots + pieces,)),
            pltpu.SemaphoreType.DMA((slots,)),
            pltpu.SemaphoreType.DMA((slots + pieces,)),
        ],
        compiler_params=pltpu.CompilerParams(
            collective_id=0, has_side_effects=True, vmem_limit_bytes=56 * 1024 * 1024
        ),
        cost_estimate=pl.CostEstimate(
            flops=ROUNDS * 2 * row_count * block_rows * (3 * width + 512),
            bytes_accessed=16 * row_count * width,
            transcendentals=ROUNDS * row_count * block_rows,
        ),
    )(
        vertex,
        vertex_state.reshape(1, row_count),
        context.reshape(pieces, CHUNK, width),
        context_state.reshape(1, block_rows),
        edge_source,
        edge_target,
    )
    vertex_out, vertex_state_out, context_out, context_state_out = pl.pallas_call(
        store_kernel,
        out_shape=tuple(jax.ShapeDtypeStruct(shape, F32) for shape in shapes),
        in_specs=[near] * 4,
        out_specs=(far,) * 4,
        scratch_shapes=[pltpu.SemaphoreType.DMA((4,))],
    )(*results)
    return (
        vertex_out,
        vertex_state_out.reshape(row_count),
        context_out.reshape(block_rows, width),
        context_state_out.reshape(block_rows),
    )


def solution(mesh):
    matrix = P(("outer", "inner"), None)
    vector = P(("outer", "inner"))
    return jax.shard_map(
        functools.partial(body, mesh.shape["outer"], mesh.shape["inner"]),
        mesh=mesh,
        in_specs=(matrix, vector, matrix, vector, matrix, matrix),
        out_specs=(matrix, vector, matrix, vector),
        check_vma=False,
    )
```

```python
import functools

import jax
import jax.numpy as jnp
from jax import lax
from jax.experimental import pallas as pl
from jax.experimental.pallas import tpu as pltpu
from jax.sharding import PartitionSpec as P

ROUNDS = 3
CHUNK = 16
DEPTH = 4

MESH = pl.DeviceIdType.MESH
BF16 = jnp.bfloat16
F32 = jnp.float32


def kernel(
    n_outer,
    n_inner,
    vertex,
    vertex_state_in,
    context,
    context_state_in,
    edge_source_in,
    edge_target_in,
    rows,
    vertex_state_out,
    context_out,
    context_state_out,
    vertex_state,
    context_state,
    edge_source,
    edge_target,
    rows_b,
    row_state,
    block,
    state,
    block_b,
    grads,
    counts,
    load_sem,
    send_sem,
    recv_sem,
    state_send_sem,
    state_recv_sem,
):
    pieces, chunk, width = context.shape
    row_count = rows.shape[0]
    block_rows = pieces * chunk
    edges = edge_source_in.shape[1] // ROUNDS
    hops = (ROUNDS - 1) * pieces

    i = lax.axis_index("inner")
    o = lax.axis_index("outer")
    right = {"inner": lax.rem(i + 1, n_inner)}
    left = {"inner": lax.rem(i + n_inner - 1, n_inner)}
    ahead = {"outer": lax.rem(o + 1, n_outer)}
    behind = {"outer": lax.rem(o + n_outer - 1, n_outer)}

    barrier = pltpu.get_barrier_semaphore()
    for neighbour in (left, right, behind, ahead):
        pl.semaphore_signal(barrier, inc=1, device_id=neighbour, device_id_type=MESH)

    small_loads = [
        pltpu.make_async_copy(source, target, load_sem.at[3 + n])
        for n, (source, target) in enumerate(
            (
                (edge_source_in, edge_source),
                (edge_target_in, edge_target),
                (vertex_state_in, vertex_state),
                (context_state_in, context_state),
            )
        )
    ]
    for load in small_loads:
        load.start()
    load_rows = pltpu.make_async_copy(vertex, rows, load_sem.at[0])
    load_first = pltpu.make_async_copy(context.at[0], block.at[0], load_sem.at[1])
    load_rest = pltpu.make_async_copy(
        context.at[pl.ds(1, pieces - 1)], block.at[pl.ds(1, pieces - 1)], load_sem.at[2]
    )
    load_rows.start()
    load_first.start()
    load_rest.start()

    def hop(s):
        return pltpu.make_async_remote_copy(
            src_ref=block.at[s],
            dst_ref=block.at[s + pieces],
            send_sem=send_sem.at[s],
            recv_sem=recv_sem.at[s + pieces],
            device_id=right,
            device_id_type=MESH,
        )

    def state_hop(s):
        return pltpu.make_async_remote_copy(
            src_ref=state.at[s],
            dst_ref=state.at[s + pieces],
            send_sem=state_send_sem.at[s],
            recv_sem=state_recv_sem.at[s + pieces],
            device_id=right,
            device_id_type=MESH,
        )

    def leave(k):
        return pltpu.make_async_remote_copy(
            src_ref=block.at[hops + k],
            dst_ref=context_out.at[k],
            send_sem=send_sem.at[hops + k],
            recv_sem=recv_sem.at[hops + pieces + k],
            device_id=ahead,
            device_id_type=MESH,
        )

    def state_leave(k):
        return pltpu.make_async_remote_copy(
            src_ref=state.at[hops + k],
            dst_ref=state.at[hops + pieces + k],
            send_sem=state_send_sem.at[hops + k],
            recv_sem=state_recv_sem.at[hops + pieces + k],
            device_id=ahead,
            device_id_type=MESH,
        )

    def count(r):
        span = pl.ds(r * edges, edges)
        target_hot = (
            edge_target[:, span] == lax.broadcasted_iota(jnp.int32, (block_rows, edges), 0)
        ).astype(F32).astype(BF16)
        source_hot = (
            edge_source[:, span] == lax.broadcasted_iota(jnp.int32, (row_count, edges), 0)
        ).astype(F32).astype(BF16)
        counts[r] = lax.dot_general(
            target_hot, source_hot, (((1,), (1,)), ((), ())), preferred_element_type=F32
        ).reshape(pieces, chunk, row_count)

    def update_chunk(slot, r, k):
        held = block[slot]
        held_b = held.astype(BF16)
        block_b[k] = held_b
        scores = lax.dot_general(
            held_b, rows_b[...], (((1,), (1,)), ((), ())), preferred_element_type=F32
        )
        prob = 1.0 / (1.0 + jnp.exp(-scores))
        grad = (prob * (1.0 / block_rows) - counts[r, k] * (1.0 - prob)).astype(BF16)
        grads[k] = grad
        chunk_grad = jnp.dot(grad, rows_b[...], preferred_element_type=F32)
        place = lax.broadcasted_iota(jnp.int32, (chunk, block_rows), 0) + k * chunk
        lane = lax.broadcasted_iota(jnp.int32, (chunk, block_rows), 1)
        mine = place == lane
        total = jnp.sum(jnp.where(mine, state[slot], 0.0), axis=1, keepdims=True)
        total = total + jnp.sum(chunk_grad * chunk_grad, axis=1, keepdims=True) * (1.0 / width)
        block[slot] = held - chunk_grad * (0.1 * lax.rsqrt(total))
        state[slot] = jnp.sum(jnp.where(mine, total, 0.0), axis=0, keepdims=True)

    def update_rows():
        rows_grad = lax.dot_general(
            grads[...].reshape(block_rows, row_count),
            block_b[...].reshape(block_rows, width),
            (((0,), (0,)), ((), ())),
            preferred_element_type=F32,
        )
        total = row_state[...] + jnp.sum(rows_grad * rows_grad, axis=1, keepdims=True) * (
            1.0 / width
        )
        row_state[...] = total
        rows[...] = rows[...] - rows_grad * (0.1 * lax.rsqrt(total))
        rows_b[...] = rows[...].astype(BF16)

    for load in small_loads:
        load.wait()
    eye = lax.broadcasted_iota(jnp.int32, (row_count, row_count), 0) == lax.broadcasted_iota(
        jnp.int32, (row_count, row_count), 1
    )
    row_state[...] = jnp.sum(jnp.where(eye, vertex_state[...], 0.0), axis=1, keepdims=True)
    for k in range(pieces):
        state[k] = context_state[...]
    count(0)
    load_rows.wait()
    rows_b[...] = rows[...].astype(BF16)
    load_first.wait()
    update_chunk(0, 0, 0)
    pl.semaphore_wait(barrier, 4)
    hop(0).start()
    state_hop(0).start()
    load_rest.wait()

    @pl.loop(1, pieces)
    def _(k):
        update_chunk(k, 0, k)

        @pl.when(k < DEPTH)
        def _():
            hop(k).start()
            state_hop(k).start()

    for r in range(1, ROUNDS):
        count(r)
    update_rows()

    for r in range(1, ROUNDS):

        @pl.loop(0, pieces)
        def _(k):
            s = (r - 1) * pieces + k
            hop(s).wait_send()
            state_hop(s).wait_send()

            @pl.when(s + DEPTH < hops)
            def _():
                hop(s + DEPTH).start()
                state_hop(s + DEPTH).start()

            hop(s).wait_recv()
            state_hop(s).wait_recv()
            update_chunk(s + pieces, r, k)
            if r == ROUNDS - 1:
                leave(k).start()
                state_leave(k).start()

        update_rows()

    vertex_state_out[...] = jnp.sum(jnp.where(eye, row_state[...], 0.0), axis=0, keepdims=True)

    @pl.loop(0, pieces)
    def _(k):
        leave(k).wait()
        state_leave(k).wait()

    context_state_out[...] = jnp.sum(state[pl.ds(hops + pieces, pieces)], axis=0)


def store_kernel(*refs):
    sources, targets, sems = refs[:4], refs[4:8], refs[8]
    copies = [
        pltpu.make_async_copy(source, target, sems.at[n])
        for n, (source, target) in enumerate(zip(sources, targets))
    ]
    for copy in copies:
        copy.start()
    for copy in copies:
        copy.wait()


def body(n_outer, n_inner, vertex, vertex_state, context, context_state, edge_source, edge_target):
    row_count, width = vertex.shape
    block_rows = context.shape[0]
    pieces = block_rows // CHUNK
    slots = ROUNDS * pieces
    far = pl.BlockSpec(memory_space=pltpu.HBM)
    near = pl.BlockSpec(memory_space=pltpu.VMEM)
    shapes = (
        (row_count, width),
        (1, row_count),
        (pieces, CHUNK, width),
        (1, block_rows),
    )
    results = pl.pallas_call(
        functools.partial(kernel, n_outer, n_inner),
        out_shape=tuple(pltpu.VMEM(shape, F32) for shape in shapes),
        in_specs=[far] * 6,
        out_specs=(near,) * 4,
        scratch_shapes=[
            pltpu.VMEM((1, row_count), F32),
            pltpu.VMEM((1, block_rows), F32),
            pltpu.VMEM(edge_source.shape, jnp.int32),
            pltpu.VMEM(edge_target.shape, jnp.int32),
            pltpu.VMEM((row_count, width), BF16),
            pltpu.VMEM((row_count, 1), F32),
            pltpu.VMEM((slots, CHUNK, width), F32),
            pltpu.VMEM((slots + pieces, 1, block_rows), F32),
            pltpu.VMEM((pieces, CHUNK, width), BF16),
            pltpu.VMEM((pieces, CHUNK, row_count), BF16),
            pltpu.VMEM((ROUNDS, pieces, CHUNK, row_count), F32),
            pltpu.SemaphoreType.DMA((7,)),
            pltpu.SemaphoreType.DMA((slots,)),
            pltpu.SemaphoreType.DMA((slots + pieces,)),
            pltpu.SemaphoreType.DMA((slots,)),
            pltpu.SemaphoreType.DMA((slots + pieces,)),
        ],
        compiler_params=pltpu.CompilerParams(
            collective_id=0, has_side_effects=True, vmem_limit_bytes=56 * 1024 * 1024
        ),
        cost_estimate=pl.CostEstimate(
            flops=ROUNDS * 2 * row_count * block_rows * (3 * width + 512),
            bytes_accessed=16 * row_count * width,
            transcendentals=ROUNDS * row_count * block_rows,
        ),
    )(
        vertex,
        vertex_state.reshape(1, row_count),
        context.reshape(pieces, CHUNK, width),
        context_state.reshape(1, block_rows),
        edge_source,
        edge_target,
    )
    vertex_out, vertex_state_out, context_out, context_state_out = pl.pallas_call(
        store_kernel,
        out_shape=tuple(jax.ShapeDtypeStruct(shape, F32) for shape in shapes),
        in_specs=[near] * 4,
        out_specs=(far,) * 4,
        scratch_shapes=[pltpu.SemaphoreType.DMA((4,))],
        compiler_params=pltpu.CompilerParams(vmem_limit_bytes=4 * 1024 * 1024),
    )(*results)
    return (
        vertex_out,
        vertex_state_out.reshape(row_count),
        context_out.reshape(block_rows, width),
        context_state_out.reshape(block_rows),
    )


def solution(mesh):
    matrix = P(("outer", "inner"), None)
    vector = P(("outer", "inner"))
    return jax.shard_map(
        functools.partial(body, mesh.shape["outer"], mesh.shape["inner"]),
        mesh=mesh,
        in_specs=(matrix, vector, matrix, vector, matrix, matrix),
        out_specs=(matrix, vector, matrix, vector),
        check_vma=False,
    )
```

```python
import functools

import jax
import jax.numpy as jnp
from jax import lax
from jax.experimental import pallas as pl
from jax.experimental.pallas import tpu as pltpu
from jax.sharding import PartitionSpec as P

ROUNDS = 3
CHUNK = 32
DEPTH = 4

MESH = pl.DeviceIdType.MESH
BF16 = jnp.bfloat16
F32 = jnp.float32


def kernel(
    n_outer,
    n_inner,
    vertex,
    vertex_state_in,
    context,
    context_state_in,
    edge_source_in,
    edge_target_in,
    rows,
    vertex_state_out,
    context_out,
    context_state_out,
    vertex_state,
    context_state,
    edge_source,
    edge_target,
    rows_b,
    row_state,
    block,
    state,
    block_b,
    grads,
    counts,
    load_sem,
    send_sem,
    recv_sem,
    state_send_sem,
    state_recv_sem,
):
    pieces, chunk, width = context.shape
    row_count = rows.shape[0]
    block_rows = pieces * chunk
    edges = edge_source_in.shape[1] // ROUNDS
    hops = (ROUNDS - 1) * pieces

    i = lax.axis_index("inner")
    o = lax.axis_index("outer")
    right = {"inner": lax.rem(i + 1, n_inner)}
    left = {"inner": lax.rem(i + n_inner - 1, n_inner)}
    ahead = {"outer": lax.rem(o + 1, n_outer)}
    behind = {"outer": lax.rem(o + n_outer - 1, n_outer)}

    barrier = pltpu.get_barrier_semaphore()
    for neighbour in (left, right, behind, ahead):
        pl.semaphore_signal(barrier, inc=1, device_id=neighbour, device_id_type=MESH)

    small_loads = [
        pltpu.make_async_copy(source, target, load_sem.at[3 + n])
        for n, (source, target) in enumerate(
            (
                (edge_source_in, edge_source),
                (edge_target_in, edge_target),
                (vertex_state_in, vertex_state),
                (context_state_in, context_state),
            )
        )
    ]
    for load in small_loads:
        load.start()
    load_rows = pltpu.make_async_copy(vertex, rows, load_sem.at[0])
    load_first = pltpu.make_async_copy(context.at[0], block.at[0], load_sem.at[1])
    load_rest = pltpu.make_async_copy(
        context.at[pl.ds(1, pieces - 1)], block.at[pl.ds(1, pieces - 1)], load_sem.at[2]
    )
    load_rows.start()
    load_first.start()
    load_rest.start()

    def hop(s):
        return pltpu.make_async_remote_copy(
            src_ref=block.at[s],
            dst_ref=block.at[s + pieces],
            send_sem=send_sem.at[s],
            recv_sem=recv_sem.at[s + pieces],
            device_id=right,
            device_id_type=MESH,
        )

    def state_move(r):
        return pltpu.make_async_remote_copy(
            src_ref=state.at[r],
            dst_ref=state.at[r + 1],
            send_sem=state_send_sem.at[r],
            recv_sem=state_recv_sem.at[r],
            device_id=ahead if r == ROUNDS - 1 else right,
            device_id_type=MESH,
        )

    def leave(k):
        return pltpu.make_async_remote_copy(
            src_ref=block.at[hops + k],
            dst_ref=context_out.at[k],
            send_sem=send_sem.at[hops + k],
            recv_sem=recv_sem.at[hops + pieces + k],
            device_id=ahead,
            device_id_type=MESH,
        )

    def count(r):
        span = pl.ds(r * edges, edges)
        target_hot = (
            edge_target[:, span] == lax.broadcasted_iota(jnp.int32, (block_rows, edges), 0)
        ).astype(F32).astype(BF16)
        source_hot = (
            edge_source[:, span] == lax.broadcasted_iota(jnp.int32, (row_count, edges), 0)
        ).astype(F32).astype(BF16)
        counts[r] = lax.dot_general(
            target_hot, source_hot, (((1,), (1,)), ((), ())), preferred_element_type=F32
        ).reshape(pieces, chunk, row_count)

    def update_chunk(slot, r, k):
        held = block[slot]
        held_b = held.astype(BF16)
        block_b[k] = held_b
        scores = lax.dot_general(
            held_b, rows_b[...], (((1,), (1,)), ((), ())), preferred_element_type=F32
        )
        prob = 1.0 / (1.0 + jnp.exp(-scores))
        grad = (prob * (1.0 / block_rows) - counts[r, k] * (1.0 - prob)).astype(BF16)
        grads[k] = grad
        chunk_grad = jnp.dot(grad, rows_b[...], preferred_element_type=F32)
        place = lax.broadcasted_iota(jnp.int32, (chunk, block_rows), 0) + k * chunk
        lane = lax.broadcasted_iota(jnp.int32, (chunk, block_rows), 1)
        mine = place == lane
        added = jnp.sum(chunk_grad * chunk_grad, axis=1, keepdims=True) * (1.0 / width)
        total = jnp.sum(jnp.where(mine, state[r], 0.0), axis=1, keepdims=True) + added
        block[slot] = held - chunk_grad * (0.1 * lax.rsqrt(total))
        state[r] += jnp.sum(jnp.where(mine, added, 0.0), axis=0, keepdims=True)

    def update_rows():
        rows_grad = lax.dot_general(
            grads[...].reshape(block_rows, row_count),
            block_b[...].reshape(block_rows, width),
            (((0,), (0,)), ((), ())),
            preferred_element_type=F32,
        )
        total = row_state[...] + jnp.sum(rows_grad * rows_grad, axis=1, keepdims=True) * (
            1.0 / width
        )
        row_state[...] = total
        rows[...] = rows[...] - rows_grad * (0.1 * lax.rsqrt(total))
        rows_b[...] = rows[...].astype(BF16)

    for load in small_loads:
        load.wait()
    eye = lax.broadcasted_iota(jnp.int32, (row_count, row_count), 0) == lax.broadcasted_iota(
        jnp.int32, (row_count, row_count), 1
    )
    row_state[...] = jnp.sum(jnp.where(eye, vertex_state[...], 0.0), axis=1, keepdims=True)
    state[0] = context_state[...]
    count(0)
    load_rows.wait()
    rows_b[...] = rows[...].astype(BF16)
    load_first.wait()
    update_chunk(0, 0, 0)
    pl.semaphore_wait(barrier, 4)
    hop(0).start()
    load_rest.wait()

    @pl.loop(1, pieces)
    def _(k):
        update_chunk(k, 0, k)

        @pl.when(k < DEPTH)
        def _():
            hop(k).start()

    state_move(0).start()
    for r in range(1, ROUNDS):
        count(r)
    update_rows()

    for r in range(1, ROUNDS):

        @pl.loop(0, pieces)
        def _(k):
            s = (r - 1) * pieces + k
            hop(s).wait_send()

            @pl.when(s + DEPTH < hops)
            def _():
                hop(s + DEPTH).start()

            hop(s).wait_recv()

            @pl.when(k == 0)
            def _():
                state_move(r - 1).wait_recv()

            update_chunk(s + pieces, r, k)
            if r == ROUNDS - 1:
                leave(k).start()

        state_move(r).start()
        update_rows()

    vertex_state_out[...] = jnp.sum(jnp.where(eye, row_state[...], 0.0), axis=0, keepdims=True)

    @pl.loop(0, pieces)
    def _(k):
        leave(k).wait()

    for r in range(ROUNDS):
        state_move(r).wait_send()
    state_move(ROUNDS - 1).wait_recv()
    context_state_out[...] = state[ROUNDS]


def store_kernel(*refs):
    sources, targets, sems = refs[:4], refs[4:8], refs[8]
    copies = [
        pltpu.make_async_copy(source, target, sems.at[n])
        for n, (source, target) in enumerate(zip(sources, targets))
    ]
    for copy in copies:
        copy.start()
    for copy in copies:
        copy.wait()


def body(n_outer, n_inner, vertex, vertex_state, context, context_state, edge_source, edge_target):
    row_count, width = vertex.shape
    block_rows = context.shape[0]
    pieces = block_rows // CHUNK
    slots = ROUNDS * pieces
    far = pl.BlockSpec(memory_space=pltpu.HBM)
    near = pl.BlockSpec(memory_space=pltpu.VMEM)
    shapes = (
        (row_count, width),
        (1, row_count),
        (pieces, CHUNK, width),
        (1, block_rows),
    )
    results = pl.pallas_call(
        functools.partial(kernel, n_outer, n_inner),
        out_shape=tuple(pltpu.VMEM(shape, F32) for shape in shapes),
        in_specs=[far] * 6,
        out_specs=(near,) * 4,
        scratch_shapes=[
            pltpu.VMEM((1, row_count), F32),
            pltpu.VMEM((1, block_rows), F32),
            pltpu.VMEM(edge_source.shape, jnp.int32),
            pltpu.VMEM(edge_target.shape, jnp.int32),
            pltpu.VMEM((row_count, width), BF16),
            pltpu.VMEM((row_count, 1), F32),
            pltpu.VMEM((slots, CHUNK, width), F32),
            pltpu.VMEM((ROUNDS + 1, 1, block_rows), F32),
            pltpu.VMEM((pieces, CHUNK, width), BF16),
            pltpu.VMEM((pieces, CHUNK, row_count), BF16),
            pltpu.VMEM((ROUNDS, pieces, CHUNK, row_count), F32),
            pltpu.SemaphoreType.DMA((7,)),
            pltpu.SemaphoreType.DMA((slots,)),
            pltpu.SemaphoreType.DMA((slots + pieces,)),
            pltpu.SemaphoreType.DMA((ROUNDS,)),
            pltpu.SemaphoreType.DMA((ROUNDS,)),
        ],
        compiler_params=pltpu.CompilerParams(
            collective_id=0, has_side_effects=True, vmem_limit_bytes=56 * 1024 * 1024
        ),
        cost_estimate=pl.CostEstimate(
            flops=ROUNDS * 2 * row_count * block_rows * (3 * width + 512),
            bytes_accessed=16 * row_count * width,
            transcendentals=ROUNDS * row_count * block_rows,
        ),
    )(
        vertex,
        vertex_state.reshape(1, row_count),
        context.reshape(pieces, CHUNK, width),
        context_state.reshape(1, block_rows),
        edge_source,
        edge_target,
    )
    vertex_out, vertex_state_out, context_out, context_state_out = pl.pallas_call(
        store_kernel,
        out_shape=tuple(jax.ShapeDtypeStruct(shape, F32) for shape in shapes),
        in_specs=[near] * 4,
        out_specs=(far,) * 4,
        scratch_shapes=[pltpu.SemaphoreType.DMA((4,))],
        compiler_params=pltpu.CompilerParams(vmem_limit_bytes=4 * 1024 * 1024),
    )(*results)
    return (
        vertex_out,
        vertex_state_out.reshape(row_count),
        context_out.reshape(block_rows, width),
        context_state_out.reshape(block_rows),
    )


def solution(mesh):
    matrix = P(("outer", "inner"), None)
    vector = P(("outer", "inner"))
    return jax.shard_map(
        functools.partial(body, mesh.shape["outer"], mesh.shape["inner"]),
        mesh=mesh,
        in_specs=(matrix, vector, matrix, vector, matrix, matrix),
        out_specs=(matrix, vector, matrix, vector),
        check_vma=False,
    )
```

```python
import functools

import jax
import jax.numpy as jnp
from jax import lax
from jax.experimental import pallas as pl
from jax.experimental.pallas import tpu as pltpu
from jax.sharding import PartitionSpec as P

ROUNDS = 3
CHUNK = 32
DEPTH = 4

MESH = pl.DeviceIdType.MESH
BF16 = jnp.bfloat16
F32 = jnp.float32


def kernel(
    n_outer,
    n_inner,
    vertex,
    vertex_state_in,
    context,
    context_state_in,
    edge_source_in,
    edge_target_in,
    rows,
    vertex_state_out,
    context_out,
    context_state_out,
    vertex_state,
    context_state,
    edge_source,
    edge_target,
    rows_b,
    rows_t,
    row_state,
    block,
    state,
    block_b,
    grads,
    counts,
    load_sem,
    send_sem,
    recv_sem,
    state_send_sem,
    state_recv_sem,
):
    pieces, chunk, width = context.shape
    row_count = rows.shape[0]
    block_rows = pieces * chunk
    edges = edge_source_in.shape[1] // ROUNDS
    hops = (ROUNDS - 1) * pieces

    i = lax.axis_index("inner")
    o = lax.axis_index("outer")
    right = {"inner": lax.rem(i + 1, n_inner)}
    left = {"inner": lax.rem(i + n_inner - 1, n_inner)}
    ahead = {"outer": lax.rem(o + 1, n_outer)}
    behind = {"outer": lax.rem(o + n_outer - 1, n_outer)}

    barrier = pltpu.get_barrier_semaphore()
    for neighbour in (left, right, behind, ahead):
        pl.semaphore_signal(barrier, inc=1, device_id=neighbour, device_id_type=MESH)

    small_loads = [
        pltpu.make_async_copy(source, target, load_sem.at[3 + n])
        for n, (source, target) in enumerate(
            (
                (edge_source_in, edge_source),
                (edge_target_in, edge_target),
                (vertex_state_in, vertex_state),
                (context_state_in, context_state),
            )
        )
    ]
    for load in small_loads:
        load.start()
    halves = [pl.ds(0, row_count // 2), pl.ds(row_count // 2, row_count // 2)]
    load_rows = [
        pltpu.make_async_copy(vertex.at[half], rows.at[half], load_sem.at[7 * n])
        for n, half in enumerate(halves)
    ]
    load_first = pltpu.make_async_copy(context.at[0], block.at[0], load_sem.at[1])
    load_rest = pltpu.make_async_copy(
        context.at[pl.ds(1, pieces - 1)], block.at[pl.ds(1, pieces - 1)], load_sem.at[2]
    )
    for load in load_rows:
        load.start()
    load_first.start()
    load_rest.start()

    def hop(s):
        return pltpu.make_async_remote_copy(
            src_ref=block.at[s],
            dst_ref=block.at[s + pieces],
            send_sem=send_sem.at[s],
            recv_sem=recv_sem.at[s + pieces],
            device_id=right,
            device_id_type=MESH,
        )

    def state_move(r):
        return pltpu.make_async_remote_copy(
            src_ref=state.at[r],
            dst_ref=state.at[r + 1],
            send_sem=state_send_sem.at[r],
            recv_sem=state_recv_sem.at[r],
            device_id=ahead if r == ROUNDS - 1 else right,
            device_id_type=MESH,
        )

    def leave(k):
        return pltpu.make_async_remote_copy(
            src_ref=block.at[hops + k],
            dst_ref=context_out.at[k],
            send_sem=send_sem.at[hops + k],
            recv_sem=recv_sem.at[hops + pieces + k],
            device_id=ahead,
            device_id_type=MESH,
        )

    def count(r):
        span = pl.ds(r * edges, edges)
        target_hot = (
            edge_target[:, span] == lax.broadcasted_iota(jnp.int32, (block_rows, edges), 0)
        ).astype(F32).astype(BF16)
        source_hot = (
            edge_source[:, span] == lax.broadcasted_iota(jnp.int32, (row_count, edges), 0)
        ).astype(F32).astype(BF16)
        counts[r] = lax.dot_general(
            target_hot, source_hot, (((1,), (1,)), ((), ())), preferred_element_type=F32
        ).reshape(pieces, chunk, row_count)

    def update_chunk(slot, r, k):
        held = block[slot]
        held_b = held.astype(BF16)
        block_b[k] = held_b
        scores = lax.dot_general(
            held_b, rows_t[...], (((1,), (0,)), ((), ())), preferred_element_type=F32
        )
        prob = 1.0 / (1.0 + jnp.exp(-scores))
        grad = (prob * (1.0 / block_rows) - counts[r, k] * (1.0 - prob)).astype(BF16)
        grads[k] = grad
        chunk_grad = jnp.dot(grad, rows_b[...], preferred_element_type=F32)
        place = lax.broadcasted_iota(jnp.int32, (chunk, block_rows), 0) + k * chunk
        lane = lax.broadcasted_iota(jnp.int32, (chunk, block_rows), 1)
        mine = place == lane
        added = jnp.sum(chunk_grad * chunk_grad, axis=1, keepdims=True) * (1.0 / width)
        total = jnp.sum(jnp.where(mine, state[r], 0.0), axis=1, keepdims=True) + added
        block[slot] = held - chunk_grad * (0.1 * lax.rsqrt(total))
        state[r] += jnp.sum(jnp.where(mine, added, 0.0), axis=0, keepdims=True)

    def round_rows():
        rounded = rows[...].astype(BF16)
        rows_b[...] = rounded
        rows_t[...] = rounded.T

    def update_rows(last):
        rows_grad = lax.dot_general(
            grads[...].reshape(block_rows, row_count),
            block_b[...].reshape(block_rows, width),
            (((0,), (0,)), ((), ())),
            preferred_element_type=F32,
        )
        total = row_state[...] + jnp.sum(rows_grad * rows_grad, axis=1, keepdims=True) * (
            1.0 / width
        )
        row_state[...] = total
        rows[...] = rows[...] - rows_grad * (0.1 * lax.rsqrt(total))
        if not last:
            round_rows()

    for load in small_loads:
        load.wait()
    state[0] = context_state[...]
    count(0)
    for load in load_rows:
        load.wait()
    round_rows()
    load_first.wait()
    update_chunk(0, 0, 0)
    pl.semaphore_wait(barrier, 4)
    hop(0).start()
    eye = lax.broadcasted_iota(jnp.int32, (row_count, row_count), 0) == lax.broadcasted_iota(
        jnp.int32, (row_count, row_count), 1
    )
    row_state[...] = jnp.sum(jnp.where(eye, vertex_state[...], 0.0), axis=1, keepdims=True)
    load_rest.wait()

    @pl.loop(1, pieces)
    def _(k):
        update_chunk(k, 0, k)

        @pl.when(k < DEPTH)
        def _():
            hop(k).start()

    state_move(0).start()
    for r in range(1, ROUNDS):
        count(r)
    update_rows(False)

    for r in range(1, ROUNDS):

        @pl.loop(0, pieces)
        def _(k):
            s = (r - 1) * pieces + k
            hop(s).wait_send()

            @pl.when(s + DEPTH < hops)
            def _():
                hop(s + DEPTH).start()

            hop(s).wait_recv()

            @pl.when(k == 0)
            def _():
                state_move(r - 1).wait_recv()

            update_chunk(s + pieces, r, k)
            if r == ROUNDS - 1:
                leave(k).start()

        state_move(r).start()
        update_rows(r == ROUNDS - 1)

    vertex_state_out[...] = jnp.sum(jnp.where(eye, row_state[...], 0.0), axis=0, keepdims=True)

    @pl.loop(0, pieces)
    def _(k):
        leave(k).wait()

    for r in range(ROUNDS):
        state_move(r).wait_send()
    state_move(ROUNDS - 1).wait_recv()
    context_state_out[...] = state[ROUNDS]


def store_kernel(*refs):
    sources, targets, sems = refs[:4], refs[4:8], refs[8]
    pairs = []
    for source, target in zip(sources, targets):
        lead = source.shape[0]
        parts = 1 if lead == 1 else 2
        for part in range(parts):
            span = pl.ds(part * (lead // parts), lead // parts)
            pairs.append((source.at[span], target.at[span]))
    copies = [
        pltpu.make_async_copy(source, target, sems.at[n])
        for n, (source, target) in enumerate(pairs)
    ]
    for copy in copies:
        copy.start()
    for copy in copies:
        copy.wait()


def body(n_outer, n_inner, vertex, vertex_state, context, context_state, edge_source, edge_target):
    row_count, width = vertex.shape
    block_rows = context.shape[0]
    pieces = block_rows // CHUNK
    slots = ROUNDS * pieces
    far = pl.BlockSpec(memory_space=pltpu.HBM)
    near = pl.BlockSpec(memory_space=pltpu.VMEM)
    shapes = (
        (row_count, width),
        (1, row_count),
        (pieces, CHUNK, width),
        (1, block_rows),
    )
    results = pl.pallas_call(
        functools.partial(kernel, n_outer, n_inner),
        out_shape=tuple(pltpu.VMEM(shape, F32) for shape in shapes),
        in_specs=[far] * 6,
        out_specs=(near,) * 4,
        scratch_shapes=[
            pltpu.VMEM((1, row_count), F32),
            pltpu.VMEM((1, block_rows), F32),
            pltpu.VMEM(edge_source.shape, jnp.int32),
            pltpu.VMEM(edge_target.shape, jnp.int32),
            pltpu.VMEM((row_count, width), BF16),
            pltpu.VMEM((width, row_count), BF16),
            pltpu.VMEM((row_count, 1), F32),
            pltpu.VMEM((slots, CHUNK, width), F32),
            pltpu.VMEM((ROUNDS + 1, 1, block_rows), F32),
            pltpu.VMEM((pieces, CHUNK, width), BF16),
            pltpu.VMEM((pieces, CHUNK, row_count), BF16),
            pltpu.VMEM((ROUNDS, pieces, CHUNK, row_count), F32),
            pltpu.SemaphoreType.DMA((8,)),
            pltpu.SemaphoreType.DMA((slots,)),
            pltpu.SemaphoreType.DMA((slots + pieces,)),
            pltpu.SemaphoreType.DMA((ROUNDS,)),
            pltpu.SemaphoreType.DMA((ROUNDS,)),
        ],
        compiler_params=pltpu.CompilerParams(
            collective_id=0, has_side_effects=True, vmem_limit_bytes=56 * 1024 * 1024
        ),
        cost_estimate=pl.CostEstimate(
            flops=ROUNDS * 2 * row_count * block_rows * (3 * width + 512),
            bytes_accessed=16 * row_count * width,
            transcendentals=ROUNDS * row_count * block_rows,
        ),
    )(
        vertex,
        vertex_state.reshape(1, row_count),
        context.reshape(pieces, CHUNK, width),
        context_state.reshape(1, block_rows),
        edge_source,
        edge_target,
    )
    vertex_out, vertex_state_out, context_out, context_state_out = pl.pallas_call(
        store_kernel,
        out_shape=tuple(jax.ShapeDtypeStruct(shape, F32) for shape in shapes),
        in_specs=[near] * 4,
        out_specs=(far,) * 4,
        scratch_shapes=[pltpu.SemaphoreType.DMA((6,))],
        compiler_params=pltpu.CompilerParams(vmem_limit_bytes=4 * 1024 * 1024),
    )(*results)
    return (
        vertex_out,
        vertex_state_out.reshape(row_count),
        context_out.reshape(block_rows, width),
        context_state_out.reshape(block_rows),
    )


def solution(mesh):
    matrix = P(("outer", "inner"), None)
    vector = P(("outer", "inner"))
    return jax.shard_map(
        functools.partial(body, mesh.shape["outer"], mesh.shape["inner"]),
        mesh=mesh,
        in_specs=(matrix, vector, matrix, vector, matrix, matrix),
        out_specs=(matrix, vector, matrix, vector),
        check_vma=False,
    )
```

```python
import functools

import jax
import jax.numpy as jnp
from jax import lax
from jax.experimental import pallas as pl
from jax.experimental.pallas import tpu as pltpu
from jax.sharding import PartitionSpec as P

ROUNDS = 3
CHUNK = 32
DEPTH = 2

MESH = pl.DeviceIdType.MESH
BF16 = jnp.bfloat16
F32 = jnp.float32


def kernel(
    n_outer,
    n_inner,
    vertex,
    vertex_state_in,
    context,
    context_state_in,
    edge_source_in,
    edge_target_in,
    rows,
    vertex_state_out,
    context_out,
    context_state_out,
    vertex_state,
    context_state,
    edge_source,
    edge_target,
    rows_b,
    rows_t,
    row_state,
    block,
    state,
    block_b,
    grads,
    counts,
    load_sem,
    send_sem,
    recv_sem,
    state_send_sem,
    state_recv_sem,
):
    pieces, chunk, width = context.shape
    row_count = rows.shape[0]
    block_rows = pieces * chunk
    edges = edge_source_in.shape[1] // ROUNDS
    hops = (ROUNDS - 1) * pieces

    i = lax.axis_index("inner")
    o = lax.axis_index("outer")
    right = {"inner": lax.rem(i + 1, n_inner)}
    left = {"inner": lax.rem(i + n_inner - 1, n_inner)}
    ahead = {"outer": lax.rem(o + 1, n_outer)}
    behind = {"outer": lax.rem(o + n_outer - 1, n_outer)}

    barrier = pltpu.get_barrier_semaphore()
    for neighbour in (left, right, behind, ahead):
        pl.semaphore_signal(barrier, inc=1, device_id=neighbour, device_id_type=MESH)

    small_loads = [
        pltpu.make_async_copy(source, target, load_sem.at[3 + n])
        for n, (source, target) in enumerate(
            (
                (edge_source_in, edge_source),
                (edge_target_in, edge_target),
                (vertex_state_in, vertex_state),
                (context_state_in, context_state),
            )
        )
    ]
    for load in small_loads:
        load.start()
    halves = [pl.ds(0, row_count // 2), pl.ds(row_count // 2, row_count // 2)]
    load_rows = [
        pltpu.make_async_copy(vertex.at[half], rows.at[half], load_sem.at[7 * n])
        for n, half in enumerate(halves)
    ]
    load_first = pltpu.make_async_copy(context.at[0], block.at[0], load_sem.at[1])
    load_rest = pltpu.make_async_copy(
        context.at[pl.ds(1, pieces - 1)], block.at[pl.ds(1, pieces - 1)], load_sem.at[2]
    )
    for load in load_rows:
        load.start()
    load_first.start()
    load_rest.start()

    def hop(s):
        return pltpu.make_async_remote_copy(
            src_ref=block.at[s],
            dst_ref=block.at[s + pieces],
            send_sem=send_sem.at[s],
            recv_sem=recv_sem.at[s + pieces],
            device_id=right,
            device_id_type=MESH,
        )

    def state_move(r):
        return pltpu.make_async_remote_copy(
            src_ref=state.at[r],
            dst_ref=state.at[r + 1],
            send_sem=state_send_sem.at[r],
            recv_sem=state_recv_sem.at[r],
            device_id=ahead if r == ROUNDS - 1 else right,
            device_id_type=MESH,
        )

    def leave(k):
        return pltpu.make_async_remote_copy(
            src_ref=block.at[hops + k],
            dst_ref=context_out.at[k],
            send_sem=send_sem.at[hops + k],
            recv_sem=recv_sem.at[hops + pieces + k],
            device_id=ahead,
            device_id_type=MESH,
        )

    def count(r):
        span = pl.ds(r * edges, edges)
        target_hot = (
            edge_target[:, span] == lax.broadcasted_iota(jnp.int32, (block_rows, edges), 0)
        ).astype(F32).astype(BF16)
        source_hot = (
            edge_source[:, span] == lax.broadcasted_iota(jnp.int32, (row_count, edges), 0)
        ).astype(F32).astype(BF16)
        counts[r] = lax.dot_general(
            target_hot, source_hot, (((1,), (1,)), ((), ())), preferred_element_type=F32
        ).reshape(pieces, chunk, row_count)

    def update_chunk(slot, r, k):
        held = block[slot]
        held_b = held.astype(BF16)
        block_b[k] = held_b
        scores = lax.dot_general(
            held_b, rows_t[...], (((1,), (0,)), ((), ())), preferred_element_type=F32
        )
        prob = 1.0 / (1.0 + jnp.exp(-scores))
        grad = (prob * (1.0 / block_rows) - counts[r, k] * (1.0 - prob)).astype(BF16)
        grads[k] = grad
        chunk_grad = jnp.dot(grad, rows_b[...], preferred_element_type=F32)
        place = lax.broadcasted_iota(jnp.int32, (chunk, block_rows), 0) + k * chunk
        lane = lax.broadcasted_iota(jnp.int32, (chunk, block_rows), 1)
        mine = place == lane
        added = jnp.sum(chunk_grad * chunk_grad, axis=1, keepdims=True) * (1.0 / width)
        total = jnp.sum(jnp.where(mine, state[r], 0.0), axis=1, keepdims=True) + added
        block[slot] = held - chunk_grad * (0.1 * lax.rsqrt(total))
        state[r] += jnp.sum(jnp.where(mine, added, 0.0), axis=0, keepdims=True)

    def round_rows():
        rounded = rows[...].astype(BF16)
        rows_b[...] = rounded
        rows_t[...] = rounded.T

    def update_rows(last):
        rows_grad = lax.dot_general(
            grads[...].reshape(block_rows, row_count),
            block_b[...].reshape(block_rows, width),
            (((0,), (0,)), ((), ())),
            preferred_element_type=F32,
        )
        total = row_state[...] + jnp.sum(rows_grad * rows_grad, axis=1, keepdims=True) * (
            1.0 / width
        )
        row_state[...] = total
        rows[...] = rows[...] - rows_grad * (0.1 * lax.rsqrt(total))
        if not last:
            round_rows()

    for load in small_loads:
        load.wait()
    state[0] = context_state[...]
    count(0)
    for load in load_rows:
        load.wait()
    round_rows()
    load_first.wait()
    update_chunk(0, 0, 0)
    pl.semaphore_wait(barrier, 4)
    hop(0).start()
    eye = lax.broadcasted_iota(jnp.int32, (row_count, row_count), 0) == lax.broadcasted_iota(
        jnp.int32, (row_count, row_count), 1
    )
    row_state[...] = jnp.sum(jnp.where(eye, vertex_state[...], 0.0), axis=1, keepdims=True)
    load_rest.wait()

    @pl.loop(1, pieces)
    def _(k):
        update_chunk(k, 0, k)

        @pl.when(k < DEPTH)
        def _():
            hop(k).start()

    state_move(0).start()
    for r in range(1, ROUNDS):
        count(r)
    update_rows(False)

    for r in range(1, ROUNDS):

        @pl.loop(0, pieces)
        def _(k):
            s = (r - 1) * pieces + k
            hop(s).wait_send()

            @pl.when(s + DEPTH < hops)
            def _():
                hop(s + DEPTH).start()

            hop(s).wait_recv()

            @pl.when(k == 0)
            def _():
                state_move(r - 1).wait_recv()

            update_chunk(s + pieces, r, k)
            if r == ROUNDS - 1:
                leave(k).start()

        state_move(r).start()
        update_rows(r == ROUNDS - 1)

    vertex_state_out[...] = jnp.sum(jnp.where(eye, row_state[...], 0.0), axis=0, keepdims=True)

    @pl.loop(0, pieces)
    def _(k):
        leave(k).wait()

    for r in range(ROUNDS):
        state_move(r).wait_send()
    state_move(ROUNDS - 1).wait_recv()
    context_state_out[...] = state[ROUNDS]


def store_kernel(*refs):
    sources, targets, sems = refs[:4], refs[4:8], refs[8]
    pairs = []
    for source, target in zip(sources, targets):
        lead = source.shape[0]
        parts = 1 if lead == 1 else 2
        for part in range(parts):
            span = pl.ds(part * (lead // parts), lead // parts)
            pairs.append((source.at[span], target.at[span]))
    copies = [
        pltpu.make_async_copy(source, target, sems.at[n])
        for n, (source, target) in enumerate(pairs)
    ]
    for copy in copies:
        copy.start()
    for copy in copies:
        copy.wait()


def body(n_outer, n_inner, vertex, vertex_state, context, context_state, edge_source, edge_target):
    row_count, width = vertex.shape
    block_rows = context.shape[0]
    pieces = block_rows // CHUNK
    slots = ROUNDS * pieces
    far = pl.BlockSpec(memory_space=pltpu.HBM)
    near = pl.BlockSpec(memory_space=pltpu.VMEM)
    shapes = (
        (row_count, width),
        (1, row_count),
        (pieces, CHUNK, width),
        (1, block_rows),
    )
    results = pl.pallas_call(
        functools.partial(kernel, n_outer, n_inner),
        out_shape=tuple(pltpu.VMEM(shape, F32) for shape in shapes),
        in_specs=[far] * 6,
        out_specs=(near,) * 4,
        scratch_shapes=[
            pltpu.VMEM((1, row_count), F32),
            pltpu.VMEM((1, block_rows), F32),
            pltpu.VMEM(edge_source.shape, jnp.int32),
            pltpu.VMEM(edge_target.shape, jnp.int32),
            pltpu.VMEM((row_count, width), BF16),
            pltpu.VMEM((width, row_count), BF16),
            pltpu.VMEM((row_count, 1), F32),
            pltpu.VMEM((slots, CHUNK, width), F32),
            pltpu.VMEM((ROUNDS + 1, 1, block_rows), F32),
            pltpu.VMEM((pieces, CHUNK, width), BF16),
            pltpu.VMEM((pieces, CHUNK, row_count), BF16),
            pltpu.VMEM((ROUNDS, pieces, CHUNK, row_count), F32),
            pltpu.SemaphoreType.DMA((8,)),
            pltpu.SemaphoreType.DMA((slots,)),
            pltpu.SemaphoreType.DMA((slots + pieces,)),
            pltpu.SemaphoreType.DMA((ROUNDS,)),
            pltpu.SemaphoreType.DMA((ROUNDS,)),
        ],
        compiler_params=pltpu.CompilerParams(
            collective_id=0, has_side_effects=True, vmem_limit_bytes=56 * 1024 * 1024
        ),
        cost_estimate=pl.CostEstimate(
            flops=ROUNDS * 2 * row_count * block_rows * (3 * width + 512),
            bytes_accessed=16 * row_count * width,
            transcendentals=ROUNDS * row_count * block_rows,
        ),
    )(
        vertex,
        vertex_state.reshape(1, row_count),
        context.reshape(pieces, CHUNK, width),
        context_state.reshape(1, block_rows),
        edge_source,
        edge_target,
    )
    vertex_out, vertex_state_out, context_out, context_state_out = pl.pallas_call(
        store_kernel,
        out_shape=tuple(jax.ShapeDtypeStruct(shape, F32) for shape in shapes),
        in_specs=[near] * 4,
        out_specs=(far,) * 4,
        scratch_shapes=[pltpu.SemaphoreType.DMA((6,))],
        compiler_params=pltpu.CompilerParams(vmem_limit_bytes=4 * 1024 * 1024),
    )(*results)
    return (
        vertex_out,
        vertex_state_out.reshape(row_count),
        context_out.reshape(block_rows, width),
        context_state_out.reshape(block_rows),
    )


def solution(mesh):
    matrix = P(("outer", "inner"), None)
    vector = P(("outer", "inner"))
    return jax.shard_map(
        functools.partial(body, mesh.shape["outer"], mesh.shape["inner"]),
        mesh=mesh,
        in_specs=(matrix, vector, matrix, vector, matrix, matrix),
        out_specs=(matrix, vector, matrix, vector),
        check_vma=False,
    )
```

```python
import functools

import jax
import jax.numpy as jnp
from jax import lax
from jax.experimental import pallas as pl
from jax.experimental.pallas import tpu as pltpu
from jax.sharding import PartitionSpec as P

ROUNDS = 3
CHUNK = 32
DEPTH = 4

MESH = pl.DeviceIdType.MESH
BF16 = jnp.bfloat16
F32 = jnp.float32


def kernel(
    n_outer,
    n_inner,
    vertex,
    vertex_state_in,
    context,
    context_state_in,
    edge_source_in,
    edge_target_in,
    rows,
    vertex_state_out,
    context_out,
    context_state_out,
    vertex_state,
    context_state,
    edge_source,
    edge_target,
    rows_b,
    rows_t,
    row_state,
    block,
    state,
    block_b,
    grads,
    counts,
    load_sem,
    send_sem,
    recv_sem,
    state_send_sem,
    state_recv_sem,
):
    pieces, chunk, width = context.shape
    row_count = rows.shape[0]
    block_rows = pieces * chunk
    edges = edge_source_in.shape[1] // ROUNDS
    hops = (ROUNDS - 1) * pieces

    i = lax.axis_index("inner")
    o = lax.axis_index("outer")
    right = {"inner": lax.rem(i + 1, n_inner)}
    left = {"inner": lax.rem(i + n_inner - 1, n_inner)}
    ahead = {"outer": lax.rem(o + 1, n_outer)}
    behind = {"outer": lax.rem(o + n_outer - 1, n_outer)}

    barrier = pltpu.get_barrier_semaphore()
    for neighbour in (left, right, behind, ahead):
        pl.semaphore_signal(barrier, inc=1, device_id=neighbour, device_id_type=MESH)

    small_loads = [
        pltpu.make_async_copy(source, target, load_sem.at[3 + n])
        for n, (source, target) in enumerate(
            (
                (edge_source_in, edge_source),
                (edge_target_in, edge_target),
                (vertex_state_in, vertex_state),
                (context_state_in, context_state),
            )
        )
    ]
    for load in small_loads:
        load.start()
    halves = [pl.ds(0, row_count // 2), pl.ds(row_count // 2, row_count // 2)]
    load_rows = [
        pltpu.make_async_copy(vertex.at[half], rows.at[half], load_sem.at[7 * n])
        for n, half in enumerate(halves)
    ]
    load_first = pltpu.make_async_copy(context.at[0], block.at[0], load_sem.at[1])
    load_rest = pltpu.make_async_copy(
        context.at[pl.ds(1, pieces - 1)], block.at[pl.ds(1, pieces - 1)], load_sem.at[2]
    )
    for load in load_rows:
        load.start()
    load_first.start()
    load_rest.start()

    def hop(s):
        return pltpu.make_async_remote_copy(
            src_ref=block.at[s],
            dst_ref=block.at[s + pieces],
            send_sem=send_sem.at[s],
            recv_sem=recv_sem.at[s + pieces],
            device_id=right,
            device_id_type=MESH,
        )

    def half_hop(h):
        span = pl.ds(h * (chunk // 2), chunk // 2)
        return pltpu.make_async_remote_copy(
            src_ref=block.at[hops - 1, span],
            dst_ref=block.at[hops - 1 + pieces, span],
            send_sem=send_sem.at[hops - 1 if h == 0 else hops + pieces],
            recv_sem=recv_sem.at[hops - 1 + pieces if h == 0 else hops + 2 * pieces],
            device_id=right,
            device_id_type=MESH,
        )

    def half_leave(h):
        span = pl.ds(h * (chunk // 2), chunk // 2)
        return pltpu.make_async_remote_copy(
            src_ref=block.at[hops - 1 + pieces, span],
            dst_ref=context_out.at[pieces - 1, span],
            send_sem=send_sem.at[hops + pieces - 1 + 2 * h],
            recv_sem=recv_sem.at[hops + 2 * pieces - 1 + 2 * h],
            device_id=ahead,
            device_id_type=MESH,
        )

    def state_move(r):
        return pltpu.make_async_remote_copy(
            src_ref=state.at[r],
            dst_ref=state.at[r + 1],
            send_sem=state_send_sem.at[r],
            recv_sem=state_recv_sem.at[r],
            device_id=ahead if r == ROUNDS - 1 else right,
            device_id_type=MESH,
        )

    def leave(k):
        return pltpu.make_async_remote_copy(
            src_ref=block.at[hops + k],
            dst_ref=context_out.at[k],
            send_sem=send_sem.at[hops + k],
            recv_sem=recv_sem.at[hops + pieces + k],
            device_id=ahead,
            device_id_type=MESH,
        )

    def count(r):
        span = pl.ds(r * edges, edges)
        target_hot = (
            edge_target[:, span] == lax.broadcasted_iota(jnp.int32, (block_rows, edges), 0)
        ).astype(F32).astype(BF16)
        source_hot = (
            edge_source[:, span] == lax.broadcasted_iota(jnp.int32, (row_count, edges), 0)
        ).astype(F32).astype(BF16)
        counts[r] = lax.dot_general(
            target_hot, source_hot, (((1,), (1,)), ((), ())), preferred_element_type=F32
        ).reshape(pieces, chunk, row_count)

    def update_chunk(slot, r, k, at=0, size=chunk):
        span = pl.ds(at, size)
        held = block[slot, span]
        held_b = held.astype(BF16)
        block_b[k, span] = held_b
        scores = lax.dot_general(
            held_b, rows_t[...], (((1,), (0,)), ((), ())), preferred_element_type=F32
        )
        prob = 1.0 / (1.0 + jnp.exp(-scores))
        grad = (prob * (1.0 / block_rows) - counts[r, k, span] * (1.0 - prob)).astype(BF16)
        grads[k, span] = grad
        chunk_grad = jnp.dot(grad, rows_b[...], preferred_element_type=F32)
        place = lax.broadcasted_iota(jnp.int32, (size, block_rows), 0) + (k * chunk + at)
        lane = lax.broadcasted_iota(jnp.int32, (size, block_rows), 1)
        mine = place == lane
        added = jnp.sum(chunk_grad * chunk_grad, axis=1, keepdims=True) * (1.0 / width)
        total = jnp.sum(jnp.where(mine, state[r], 0.0), axis=1, keepdims=True) + added
        block[slot, span] = held - chunk_grad * (0.1 * lax.rsqrt(total))
        state[r] += jnp.sum(jnp.where(mine, added, 0.0), axis=0, keepdims=True)

    def round_rows():
        rounded = rows[...].astype(BF16)
        rows_b[...] = rounded
        rows_t[...] = rounded.T

    def update_rows(last):
        rows_grad = lax.dot_general(
            grads[...].reshape(block_rows, row_count),
            block_b[...].reshape(block_rows, width),
            (((0,), (0,)), ((), ())),
            preferred_element_type=F32,
        )
        total = row_state[...] + jnp.sum(rows_grad * rows_grad, axis=1, keepdims=True) * (
            1.0 / width
        )
        row_state[...] = total
        rows[...] = rows[...] - rows_grad * (0.1 * lax.rsqrt(total))
        if not last:
            round_rows()

    for load in small_loads:
        load.wait()
    state[0] = context_state[...]
    count(0)
    for load in load_rows:
        load.wait()
    round_rows()
    load_first.wait()
    update_chunk(0, 0, 0)
    pl.semaphore_wait(barrier, 4)
    hop(0).start()
    eye = lax.broadcasted_iota(jnp.int32, (row_count, row_count), 0) == lax.broadcasted_iota(
        jnp.int32, (row_count, row_count), 1
    )
    row_state[...] = jnp.sum(jnp.where(eye, vertex_state[...], 0.0), axis=1, keepdims=True)
    load_rest.wait()

    @pl.loop(1, pieces)
    def _(k):
        update_chunk(k, 0, k)

        @pl.when(k < DEPTH)
        def _():
            hop(k).start()

    state_move(0).start()
    for r in range(1, ROUNDS):
        count(r)
    update_rows(False)

    for r in range(1, ROUNDS):

        last = r == ROUNDS - 1

        @pl.loop(0, pieces - 1 if last else pieces)
        def _(k):
            s = (r - 1) * pieces + k
            hop(s).wait_send()

            @pl.when(s + DEPTH < hops - 1)
            def _():
                hop(s + DEPTH).start()

            @pl.when(s + DEPTH == hops - 1)
            def _():
                half_hop(0).start()
                half_hop(1).start()

            hop(s).wait_recv()

            @pl.when(k == 0)
            def _():
                state_move(r - 1).wait_recv()

            update_chunk(s + pieces, r, k)
            if last:
                leave(k).start()

        if last:
            for h in range(2):
                half_hop(h).wait()
                update_chunk(hops - 1 + pieces, r, pieces - 1, h * (chunk // 2), chunk // 2)
                half_leave(h).start()
        state_move(r).start()
        update_rows(last)

    vertex_state_out[...] = jnp.sum(jnp.where(eye, row_state[...], 0.0), axis=0, keepdims=True)

    @pl.loop(0, pieces - 1)
    def _(k):
        leave(k).wait()

    for h in range(2):
        half_leave(h).wait()

    for r in range(ROUNDS):
        state_move(r).wait_send()
    state_move(ROUNDS - 1).wait_recv()
    context_state_out[...] = state[ROUNDS]


def store_kernel(*refs):
    sources, targets, sems = refs[:4], refs[4:8], refs[8]
    pairs = []
    for source, target in zip(sources, targets):
        lead = source.shape[0]
        parts = 1 if lead == 1 else 2
        for part in range(parts):
            span = pl.ds(part * (lead // parts), lead // parts)
            pairs.append((source.at[span], target.at[span]))
    copies = [
        pltpu.make_async_copy(source, target, sems.at[n])
        for n, (source, target) in enumerate(pairs)
    ]
    for copy in copies:
        copy.start()
    for copy in copies:
        copy.wait()


def body(n_outer, n_inner, vertex, vertex_state, context, context_state, edge_source, edge_target):
    row_count, width = vertex.shape
    block_rows = context.shape[0]
    pieces = block_rows // CHUNK
    slots = ROUNDS * pieces
    far = pl.BlockSpec(memory_space=pltpu.HBM)
    near = pl.BlockSpec(memory_space=pltpu.VMEM)
    shapes = (
        (row_count, width),
        (1, row_count),
        (pieces, CHUNK, width),
        (1, block_rows),
    )
    results = pl.pallas_call(
        functools.partial(kernel, n_outer, n_inner),
        out_shape=tuple(pltpu.VMEM(shape, F32) for shape in shapes),
        in_specs=[far] * 6,
        out_specs=(near,) * 4,
        scratch_shapes=[
            pltpu.VMEM((1, row_count), F32),
            pltpu.VMEM((1, block_rows), F32),
            pltpu.VMEM(edge_source.shape, jnp.int32),
            pltpu.VMEM(edge_target.shape, jnp.int32),
            pltpu.VMEM((row_count, width), BF16),
            pltpu.VMEM((width, row_count), BF16),
            pltpu.VMEM((row_count, 1), F32),
            pltpu.VMEM((slots, CHUNK, width), F32),
            pltpu.VMEM((ROUNDS + 1, 1, block_rows), F32),
            pltpu.VMEM((pieces, CHUNK, width), BF16),
            pltpu.VMEM((pieces, CHUNK, row_count), BF16),
            pltpu.VMEM((ROUNDS, pieces, CHUNK, row_count), F32),
            pltpu.SemaphoreType.DMA((8,)),
            pltpu.SemaphoreType.DMA((slots + 2,)),
            pltpu.SemaphoreType.DMA((slots + pieces + 2,)),
            pltpu.SemaphoreType.DMA((ROUNDS,)),
            pltpu.SemaphoreType.DMA((ROUNDS,)),
        ],
        compiler_params=pltpu.CompilerParams(
            collective_id=0, has_side_effects=True, vmem_limit_bytes=56 * 1024 * 1024
        ),
        cost_estimate=pl.CostEstimate(
            flops=ROUNDS * 2 * row_count * block_rows * (3 * width + 512),
            bytes_accessed=16 * row_count * width,
            transcendentals=ROUNDS * row_count * block_rows,
        ),
    )(
        vertex,
        vertex_state.reshape(1, row_count),
        context.reshape(pieces, CHUNK, width),
        context_state.reshape(1, block_rows),
        edge_source,
        edge_target,
    )
    vertex_out, vertex_state_out, context_out, context_state_out = pl.pallas_call(
        store_kernel,
        out_shape=tuple(jax.ShapeDtypeStruct(shape, F32) for shape in shapes),
        in_specs=[near] * 4,
        out_specs=(far,) * 4,
        scratch_shapes=[pltpu.SemaphoreType.DMA((6,))],
        compiler_params=pltpu.CompilerParams(vmem_limit_bytes=4 * 1024 * 1024),
    )(*results)
    return (
        vertex_out,
        vertex_state_out.reshape(row_count),
        context_out.reshape(block_rows, width),
        context_state_out.reshape(block_rows),
    )


def solution(mesh):
    matrix = P(("outer", "inner"), None)
    vector = P(("outer", "inner"))
    return jax.shard_map(
        functools.partial(body, mesh.shape["outer"], mesh.shape["inner"]),
        mesh=mesh,
        in_specs=(matrix, vector, matrix, vector, matrix, matrix),
        out_specs=(matrix, vector, matrix, vector),
        check_vma=False,
    )
```

```python
import functools

import jax
import jax.numpy as jnp
from jax import lax
from jax.experimental import pallas as pl
from jax.experimental.pallas import tpu as pltpu
from jax.sharding import PartitionSpec as P

ROUNDS = 3
CHUNK = 32
DEPTH = 4

MESH = pl.DeviceIdType.MESH
BF16 = jnp.bfloat16
F32 = jnp.float32


def kernel(
    n_outer,
    n_inner,
    vertex,
    vertex_state_in,
    context,
    context_state_in,
    edge_source_in,
    edge_target_in,
    rows,
    vertex_state_out,
    context_out,
    context_state_out,
    vertex_state,
    context_state,
    edge_source,
    edge_target,
    rows_b,
    rows_t,
    row_state,
    block,
    state,
    block_b,
    grads,
    counts,
    load_sem,
    send_sem,
    recv_sem,
    state_send_sem,
    state_recv_sem,
):
    pieces, chunk, width = context.shape
    row_count = rows.shape[0]
    block_rows = pieces * chunk
    edges = edge_source_in.shape[1] // ROUNDS
    hops = (ROUNDS - 1) * pieces

    i = lax.axis_index("inner")
    o = lax.axis_index("outer")
    right = {"inner": lax.rem(i + 1, n_inner)}
    left = {"inner": lax.rem(i + n_inner - 1, n_inner)}
    ahead = {"outer": lax.rem(o + 1, n_outer)}
    behind = {"outer": lax.rem(o + n_outer - 1, n_outer)}

    small_loads = [
        pltpu.make_async_copy(source, target, load_sem.at[3 + n])
        for n, (source, target) in enumerate(
            (
                (edge_source_in, edge_source),
                (edge_target_in, edge_target),
                (vertex_state_in, vertex_state),
                (context_state_in, context_state),
            )
        )
    ]
    for load in small_loads:
        load.start()
    halves = [pl.ds(0, row_count // 2), pl.ds(row_count // 2, row_count // 2)]
    load_rows = [
        pltpu.make_async_copy(vertex.at[half], rows.at[half], load_sem.at[7 * n])
        for n, half in enumerate(halves)
    ]
    load_first = pltpu.make_async_copy(context.at[0], block.at[0], load_sem.at[1])
    load_rest = pltpu.make_async_copy(
        context.at[pl.ds(1, pieces - 1)], block.at[pl.ds(1, pieces - 1)], load_sem.at[2]
    )
    for load in load_rows:
        load.start()
    load_first.start()
    load_rest.start()

    barrier = pltpu.get_barrier_semaphore()
    for neighbour in (left, right, behind, ahead):
        pl.semaphore_signal(barrier, inc=1, device_id=neighbour, device_id_type=MESH)

    def hop(s):
        return pltpu.make_async_remote_copy(
            src_ref=block.at[s],
            dst_ref=block.at[s + pieces],
            send_sem=send_sem.at[s],
            recv_sem=recv_sem.at[s + pieces],
            device_id=right,
            device_id_type=MESH,
        )

    def half_hop(h):
        span = pl.ds(h * (chunk // 2), chunk // 2)
        return pltpu.make_async_remote_copy(
            src_ref=block.at[hops - 1, span],
            dst_ref=block.at[hops - 1 + pieces, span],
            send_sem=send_sem.at[hops - 1 if h == 0 else hops + pieces],
            recv_sem=recv_sem.at[hops - 1 + pieces if h == 0 else hops + 2 * pieces],
            device_id=right,
            device_id_type=MESH,
        )

    def half_leave(h):
        span = pl.ds(h * (chunk // 2), chunk // 2)
        return pltpu.make_async_remote_copy(
            src_ref=block.at[hops - 1 + pieces, span],
            dst_ref=context_out.at[pieces - 1, span],
            send_sem=send_sem.at[hops + pieces - 1 + 2 * h],
            recv_sem=recv_sem.at[hops + 2 * pieces - 1 + 2 * h],
            device_id=ahead,
            device_id_type=MESH,
        )

    def state_move(r):
        return pltpu.make_async_remote_copy(
            src_ref=state.at[r],
            dst_ref=state.at[r + 1],
            send_sem=state_send_sem.at[r],
            recv_sem=state_recv_sem.at[r],
            device_id=ahead if r == ROUNDS - 1 else right,
            device_id_type=MESH,
        )

    def leave(k):
        return pltpu.make_async_remote_copy(
            src_ref=block.at[hops + k],
            dst_ref=context_out.at[k],
            send_sem=send_sem.at[hops + k],
            recv_sem=recv_sem.at[hops + pieces + k],
            device_id=ahead,
            device_id_type=MESH,
        )

    def count(r, first, number):
        span = pl.ds(r * edges, edges)
        target_hot = (
            edge_target[:, span]
            == lax.broadcasted_iota(jnp.int32, (number * chunk, edges), 0) + first * chunk
        ).astype(F32).astype(BF16)
        source_hot = (
            edge_source[:, span] == lax.broadcasted_iota(jnp.int32, (row_count, edges), 0)
        ).astype(F32).astype(BF16)
        counts[r, pl.ds(first, number)] = lax.dot_general(
            target_hot, source_hot, (((1,), (1,)), ((), ())), preferred_element_type=F32
        ).reshape(number, chunk, row_count)

    def update_chunk(slot, r, k, at=0, size=chunk):
        span = pl.ds(at, size)
        held = block[slot, span]
        held_b = held.astype(BF16)
        block_b[k, span] = held_b
        scores = lax.dot_general(
            held_b, rows_t[...], (((1,), (0,)), ((), ())), preferred_element_type=F32
        )
        prob = 1.0 / (1.0 + jnp.exp(-scores))
        grad = (prob * (1.0 / block_rows) - counts[r, k, span] * (1.0 - prob)).astype(BF16)
        grads[k, span] = grad
        chunk_grad = jnp.dot(grad, rows_b[...], preferred_element_type=F32)
        place = lax.broadcasted_iota(jnp.int32, (size, block_rows), 0) + (k * chunk + at)
        lane = lax.broadcasted_iota(jnp.int32, (size, block_rows), 1)
        mine = place == lane
        added = jnp.sum(chunk_grad * chunk_grad, axis=1, keepdims=True) * (1.0 / width)
        total = jnp.sum(jnp.where(mine, state[r], 0.0), axis=1, keepdims=True) + added
        block[slot, span] = held - chunk_grad * (0.1 * lax.rsqrt(total))
        state[r] += jnp.sum(jnp.where(mine, added, 0.0), axis=0, keepdims=True)

    def round_rows(half):
        rounded = rows[half].astype(BF16)
        rows_b[half] = rounded
        rows_t[:, half] = rounded.T

    def update_rows(last):
        rows_grad = lax.dot_general(
            grads[...].reshape(block_rows, row_count),
            block_b[...].reshape(block_rows, width),
            (((0,), (0,)), ((), ())),
            preferred_element_type=F32,
        )
        total = row_state[...] + jnp.sum(rows_grad * rows_grad, axis=1, keepdims=True) * (
            1.0 / width
        )
        row_state[...] = total
        rows[...] = rows[...] - rows_grad * (0.1 * lax.rsqrt(total))
        if not last:
            for half in halves:
                round_rows(half)

    for load in small_loads:
        load.wait()
    state[0] = context_state[...]
    count(0, 0, 1)
    for half, load in zip(halves, load_rows):
        load.wait()
        round_rows(half)
    load_first.wait()
    update_chunk(0, 0, 0)
    pl.semaphore_wait(barrier, 4)
    hop(0).start()
    count(0, 1, pieces - 1)
    eye = lax.broadcasted_iota(jnp.int32, (row_count, row_count), 0) == lax.broadcasted_iota(
        jnp.int32, (row_count, row_count), 1
    )
    row_state[...] = jnp.sum(jnp.where(eye, vertex_state[...], 0.0), axis=1, keepdims=True)
    load_rest.wait()

    @pl.loop(1, pieces)
    def _(k):
        update_chunk(k, 0, k)

        @pl.when(k < DEPTH)
        def _():
            hop(k).start()

    state_move(0).start()
    for r in range(1, ROUNDS):
        count(r, 0, pieces)
    update_rows(False)

    for r in range(1, ROUNDS):

        last = r == ROUNDS - 1

        @pl.loop(0, pieces - 1 if last else pieces)
        def _(k):
            s = (r - 1) * pieces + k
            hop(s).wait_send()

            @pl.when(s + DEPTH < hops - 1)
            def _():
                hop(s + DEPTH).start()

            @pl.when(s + DEPTH == hops - 1)
            def _():
                half_hop(0).start()
                half_hop(1).start()

            hop(s).wait_recv()

            @pl.when(k == 0)
            def _():
                state_move(r - 1).wait_recv()

            update_chunk(s + pieces, r, k)
            if last:
                leave(k).start()

        if last:
            for h in range(2):
                half_hop(h).wait()
                update_chunk(hops - 1 + pieces, r, pieces - 1, h * (chunk // 2), chunk // 2)
                half_leave(h).start()
        state_move(r).start()
        update_rows(last)

    vertex_state_out[...] = jnp.sum(jnp.where(eye, row_state[...], 0.0), axis=0, keepdims=True)

    @pl.loop(0, pieces - 1)
    def _(k):
        leave(k).wait()

    for h in range(2):
        half_leave(h).wait()

    for r in range(ROUNDS):
        state_move(r).wait_send()
    state_move(ROUNDS - 1).wait_recv()
    context_state_out[...] = state[ROUNDS]


def store_kernel(*refs):
    sources, targets, sems = refs[:4], refs[4:8], refs[8]
    pairs = []
    for source, target in zip(sources, targets):
        lead = source.shape[0]
        parts = 1 if lead == 1 else 2
        for part in range(parts):
            span = pl.ds(part * (lead // parts), lead // parts)
            pairs.append((source.at[span], target.at[span]))
    copies = [
        pltpu.make_async_copy(source, target, sems.at[n])
        for n, (source, target) in enumerate(pairs)
    ]
    for copy in copies:
        copy.start()
    for copy in copies:
        copy.wait()


def body(n_outer, n_inner, vertex, vertex_state, context, context_state, edge_source, edge_target):
    row_count, width = vertex.shape
    block_rows = context.shape[0]
    pieces = block_rows // CHUNK
    slots = ROUNDS * pieces
    far = pl.BlockSpec(memory_space=pltpu.HBM)
    near = pl.BlockSpec(memory_space=pltpu.VMEM)
    shapes = (
        (row_count, width),
        (1, row_count),
        (pieces, CHUNK, width),
        (1, block_rows),
    )
    results = pl.pallas_call(
        functools.partial(kernel, n_outer, n_inner),
        out_shape=tuple(pltpu.VMEM(shape, F32) for shape in shapes),
        in_specs=[far] * 6,
        out_specs=(near,) * 4,
        scratch_shapes=[
            pltpu.VMEM((1, row_count), F32),
            pltpu.VMEM((1, block_rows), F32),
            pltpu.VMEM(edge_source.shape, jnp.int32),
            pltpu.VMEM(edge_target.shape, jnp.int32),
            pltpu.VMEM((row_count, width), BF16),
            pltpu.VMEM((width, row_count), BF16),
            pltpu.VMEM((row_count, 1), F32),
            pltpu.VMEM((slots, CHUNK, width), F32),
            pltpu.VMEM((ROUNDS + 1, 1, block_rows), F32),
            pltpu.VMEM((pieces, CHUNK, width), BF16),
            pltpu.VMEM((pieces, CHUNK, row_count), BF16),
            pltpu.VMEM((ROUNDS, pieces, CHUNK, row_count), F32),
            pltpu.SemaphoreType.DMA((8,)),
            pltpu.SemaphoreType.DMA((slots + 2,)),
            pltpu.SemaphoreType.DMA((slots + pieces + 2,)),
            pltpu.SemaphoreType.DMA((ROUNDS,)),
            pltpu.SemaphoreType.DMA((ROUNDS,)),
        ],
        compiler_params=pltpu.CompilerParams(
            collective_id=0, has_side_effects=True, vmem_limit_bytes=56 * 1024 * 1024
        ),
        cost_estimate=pl.CostEstimate(
            flops=ROUNDS * 2 * row_count * block_rows * (3 * width + 512),
            bytes_accessed=16 * row_count * width,
            transcendentals=ROUNDS * row_count * block_rows,
        ),
    )(
        vertex,
        vertex_state.reshape(1, row_count),
        context.reshape(pieces, CHUNK, width),
        context_state.reshape(1, block_rows),
        edge_source,
        edge_target,
    )
    vertex_out, vertex_state_out, context_out, context_state_out = pl.pallas_call(
        store_kernel,
        out_shape=tuple(jax.ShapeDtypeStruct(shape, F32) for shape in shapes),
        in_specs=[near] * 4,
        out_specs=(far,) * 4,
        scratch_shapes=[pltpu.SemaphoreType.DMA((6,))],
        compiler_params=pltpu.CompilerParams(vmem_limit_bytes=4 * 1024 * 1024),
    )(*results)
    return (
        vertex_out,
        vertex_state_out.reshape(row_count),
        context_out.reshape(block_rows, width),
        context_state_out.reshape(block_rows),
    )


def solution(mesh):
    matrix = P(("outer", "inner"), None)
    vector = P(("outer", "inner"))
    return jax.shard_map(
        functools.partial(body, mesh.shape["outer"], mesh.shape["inner"]),
        mesh=mesh,
        in_specs=(matrix, vector, matrix, vector, matrix, matrix),
        out_specs=(matrix, vector, matrix, vector),
        check_vma=False,
    )
```

```python
import functools

import jax
import jax.numpy as jnp
from jax import lax
from jax.experimental import pallas as pl
from jax.experimental.pallas import tpu as pltpu
from jax.sharding import PartitionSpec as P

ROUNDS = 3
CHUNK = 64
DEPTH = 2

MESH = pl.DeviceIdType.MESH
BF16 = jnp.bfloat16
F32 = jnp.float32


def kernel(
    n_outer,
    n_inner,
    vertex,
    vertex_state_in,
    context,
    context_state_in,
    edge_source_in,
    edge_target_in,
    rows,
    vertex_state_out,
    context_out,
    context_state_out,
    vertex_state,
    context_state,
    edge_source,
    edge_target,
    rows_b,
    rows_t,
    row_state,
    block,
    state,
    block_b,
    grads,
    counts,
    load_sem,
    send_sem,
    recv_sem,
    state_send_sem,
    state_recv_sem,
):
    pieces, chunk, width = context.shape
    row_count = rows.shape[0]
    block_rows = pieces * chunk
    edges = edge_source_in.shape[1] // ROUNDS
    hops = (ROUNDS - 1) * pieces
    slots = ROUNDS * pieces
    parts = ((0, chunk // 2), (chunk // 2, chunk // 4), (3 * chunk // 4, chunk // 4))

    i = lax.axis_index("inner")
    o = lax.axis_index("outer")
    right = {"inner": lax.rem(i + 1, n_inner)}
    left = {"inner": lax.rem(i + n_inner - 1, n_inner)}
    ahead = {"outer": lax.rem(o + 1, n_outer)}
    behind = {"outer": lax.rem(o + n_outer - 1, n_outer)}

    small_loads = [
        pltpu.make_async_copy(source, target, load_sem.at[3 + n])
        for n, (source, target) in enumerate(
            (
                (edge_source_in, edge_source),
                (edge_target_in, edge_target),
                (vertex_state_in, vertex_state),
                (context_state_in, context_state),
            )
        )
    ]
    for load in small_loads:
        load.start()
    halves = [pl.ds(0, row_count // 2), pl.ds(row_count // 2, row_count // 2)]
    load_rows = [
        pltpu.make_async_copy(vertex.at[half], rows.at[half], load_sem.at[7 * n])
        for n, half in enumerate(halves)
    ]
    load_first = pltpu.make_async_copy(context.at[0], block.at[0], load_sem.at[1])
    load_rest = pltpu.make_async_copy(
        context.at[pl.ds(1, pieces - 1)], block.at[pl.ds(1, pieces - 1)], load_sem.at[2]
    )
    for load in load_rows:
        load.start()
    load_first.start()
    load_rest.start()

    barrier = pltpu.get_barrier_semaphore()
    for neighbour in (left, behind):
        pl.semaphore_signal(barrier, inc=1, device_id=neighbour, device_id_type=MESH)

    def hop(s):
        return pltpu.make_async_remote_copy(
            src_ref=block.at[s],
            dst_ref=block.at[s + pieces],
            send_sem=send_sem.at[s],
            recv_sem=recv_sem.at[s + pieces],
            device_id=right,
            device_id_type=MESH,
        )

    def part_hop(h):
        span = pl.ds(*parts[h])
        return pltpu.make_async_remote_copy(
            src_ref=block.at[hops - 1, span],
            dst_ref=block.at[hops - 1 + pieces, span],
            send_sem=send_sem.at[hops - 1 if h == 0 else slots + h - 1],
            recv_sem=recv_sem.at[slots - 1 if h == 0 else slots + pieces + h - 1],
            device_id=right,
            device_id_type=MESH,
        )

    def part_leave(h):
        span = pl.ds(*parts[h])
        return pltpu.make_async_remote_copy(
            src_ref=block.at[hops - 1 + pieces, span],
            dst_ref=context_out.at[pieces - 1, span],
            send_sem=send_sem.at[slots - 1 if h == 0 else slots + h + 1],
            recv_sem=recv_sem.at[slots + pieces - 1 if h == 0 else slots + pieces + h + 1],
            device_id=ahead,
            device_id_type=MESH,
        )

    def state_move(r):
        return pltpu.make_async_remote_copy(
            src_ref=state.at[r],
            dst_ref=state.at[r + 1],
            send_sem=state_send_sem.at[r],
            recv_sem=state_recv_sem.at[r],
            device_id=ahead if r == ROUNDS - 1 else right,
            device_id_type=MESH,
        )

    def leave(k):
        return pltpu.make_async_remote_copy(
            src_ref=block.at[hops + k],
            dst_ref=context_out.at[k],
            send_sem=send_sem.at[hops + k],
            recv_sem=recv_sem.at[hops + pieces + k],
            device_id=ahead,
            device_id_type=MESH,
        )

    def count(r, first, number):
        span = pl.ds(r * edges, edges)
        target_hot = (
            edge_target[:, span]
            == lax.broadcasted_iota(jnp.int32, (number * chunk, edges), 0) + first * chunk
        ).astype(F32).astype(BF16)
        source_hot = (
            edge_source[:, span] == lax.broadcasted_iota(jnp.int32, (row_count, edges), 0)
        ).astype(F32).astype(BF16)
        counts[r, pl.ds(first, number)] = lax.dot_general(
            target_hot, source_hot, (((1,), (1,)), ((), ())), preferred_element_type=F32
        ).reshape(number, chunk, row_count)

    def update_chunk(slot, r, k, at=0, size=chunk):
        span = pl.ds(at, size)
        held = block[slot, span]
        held_b = held.astype(BF16)
        block_b[k, span] = held_b
        scores = lax.dot_general(
            held_b, rows_t[...], (((1,), (0,)), ((), ())), preferred_element_type=F32
        )
        prob = 1.0 / (1.0 + jnp.exp(-scores))
        grad = (prob * (1.0 / block_rows) - counts[r, k, span] * (1.0 - prob)).astype(BF16)
        grads[k, span] = grad
        chunk_grad = jnp.dot(grad, rows_b[...], preferred_element_type=F32)
        place = lax.broadcasted_iota(jnp.int32, (size, block_rows), 0) + (k * chunk + at)
        lane = lax.broadcasted_iota(jnp.int32, (size, block_rows), 1)
        mine = place == lane
        added = jnp.sum(chunk_grad * chunk_grad, axis=1, keepdims=True) * (1.0 / width)
        total = jnp.sum(jnp.where(mine, state[r], 0.0), axis=1, keepdims=True) + added
        block[slot, span] = held - chunk_grad * (0.1 * lax.rsqrt(total))
        state[r] += jnp.sum(jnp.where(mine, added, 0.0), axis=0, keepdims=True)

    def round_rows(half):
        rounded = rows[half].astype(BF16)
        rows_b[half] = rounded
        rows_t[:, half] = rounded.T

    def update_rows(last):
        rows_grad = lax.dot_general(
            grads[...].reshape(block_rows, row_count),
            block_b[...].reshape(block_rows, width),
            (((0,), (0,)), ((), ())),
            preferred_element_type=F32,
        )
        total = row_state[...] + jnp.sum(rows_grad * rows_grad, axis=1, keepdims=True) * (
            1.0 / width
        )
        row_state[...] = total
        rows[...] = rows[...] - rows_grad * (0.1 * lax.rsqrt(total))
        if not last:
            for half in halves:
                round_rows(half)

    for load in small_loads:
        load.wait()
    state[0] = context_state[...]
    count(0, 0, 1)
    for half, load in zip(halves, load_rows):
        load.wait()
        round_rows(half)
    load_first.wait()
    update_chunk(0, 0, 0)
    pl.semaphore_wait(barrier, 2)
    hop(0).start()
    count(0, 1, pieces - 1)
    eye = lax.broadcasted_iota(jnp.int32, (row_count, row_count), 0) == lax.broadcasted_iota(
        jnp.int32, (row_count, row_count), 1
    )
    row_state[...] = jnp.sum(jnp.where(eye, vertex_state[...], 0.0), axis=1, keepdims=True)
    load_rest.wait()

    @pl.loop(1, pieces)
    def _(k):
        update_chunk(k, 0, k)

        @pl.when(k < DEPTH)
        def _():
            hop(k).start()

    state_move(0).start()
    for r in range(1, ROUNDS):
        count(r, 0, pieces)
    update_rows(False)

    for r in range(1, ROUNDS):

        last = r == ROUNDS - 1

        @pl.loop(0, pieces - 1 if last else pieces)
        def _(k):
            s = (r - 1) * pieces + k
            hop(s).wait_send()

            @pl.when(s + DEPTH < hops - 1)
            def _():
                hop(s + DEPTH).start()

            @pl.when(s + DEPTH == hops - 1)
            def _():
                for h in range(len(parts)):
                    part_hop(h).start()

            hop(s).wait_recv()

            @pl.when(k == 0)
            def _():
                state_move(r - 1).wait_recv()

            update_chunk(s + pieces, r, k)
            if last:
                leave(k).start()

        if last:
            for h in range(len(parts)):
                part_hop(h).wait()
                update_chunk(hops - 1 + pieces, r, pieces - 1, *parts[h])
                part_leave(h).start()
        state_move(r).start()
        update_rows(last)

    vertex_state_out[...] = jnp.sum(jnp.where(eye, row_state[...], 0.0), axis=0, keepdims=True)

    @pl.loop(0, pieces - 1)
    def _(k):
        leave(k).wait()

    for h in range(len(parts)):
        part_leave(h).wait()

    for r in range(ROUNDS):
        state_move(r).wait_send()
    state_move(ROUNDS - 1).wait_recv()
    context_state_out[...] = state[ROUNDS]


def store_kernel(*refs):
    sources, targets, sems = refs[:4], refs[4:8], refs[8]
    pairs = []
    for source, target in zip(sources, targets):
        lead = source.shape[0]
        parts = 1 if lead == 1 else 2
        for part in range(parts):
            span = pl.ds(part * (lead // parts), lead // parts)
            pairs.append((source.at[span], target.at[span]))
    copies = [
        pltpu.make_async_copy(source, target, sems.at[n])
        for n, (source, target) in enumerate(pairs)
    ]
    for copy in copies:
        copy.start()
    for copy in copies:
        copy.wait()


def body(n_outer, n_inner, vertex, vertex_state, context, context_state, edge_source, edge_target):
    row_count, width = vertex.shape
    block_rows = context.shape[0]
    pieces = block_rows // CHUNK
    slots = ROUNDS * pieces
    far = pl.BlockSpec(memory_space=pltpu.HBM)
    near = pl.BlockSpec(memory_space=pltpu.VMEM)
    shapes = (
        (row_count, width),
        (1, row_count),
        (pieces, CHUNK, width),
        (1, block_rows),
    )
    results = pl.pallas_call(
        functools.partial(kernel, n_outer, n_inner),
        out_shape=tuple(pltpu.VMEM(shape, F32) for shape in shapes),
        in_specs=[far] * 6,
        out_specs=(near,) * 4,
        scratch_shapes=[
            pltpu.VMEM((1, row_count), F32),
            pltpu.VMEM((1, block_rows), F32),
            pltpu.VMEM(edge_source.shape, jnp.int32),
            pltpu.VMEM(edge_target.shape, jnp.int32),
            pltpu.VMEM((row_count, width), BF16),
            pltpu.VMEM((width, row_count), BF16),
            pltpu.VMEM((row_count, 1), F32),
            pltpu.VMEM((slots, CHUNK, width), F32),
            pltpu.VMEM((ROUNDS + 1, 1, block_rows), F32),
            pltpu.VMEM((pieces, CHUNK, width), BF16),
            pltpu.VMEM((pieces, CHUNK, row_count), BF16),
            pltpu.VMEM((ROUNDS, pieces, CHUNK, row_count), F32),
            pltpu.SemaphoreType.DMA((8,)),
            pltpu.SemaphoreType.DMA((slots + 4,)),
            pltpu.SemaphoreType.DMA((slots + pieces + 4,)),
            pltpu.SemaphoreType.DMA((ROUNDS,)),
            pltpu.SemaphoreType.DMA((ROUNDS,)),
        ],
        compiler_params=pltpu.CompilerParams(
            collective_id=0, has_side_effects=True, vmem_limit_bytes=56 * 1024 * 1024
        ),
        cost_estimate=pl.CostEstimate(
            flops=ROUNDS * 2 * row_count * block_rows * (3 * width + 512),
            bytes_accessed=16 * row_count * width,
            transcendentals=ROUNDS * row_count * block_rows,
        ),
    )(
        vertex,
        vertex_state.reshape(1, row_count),
        context.reshape(pieces, CHUNK, width),
        context_state.reshape(1, block_rows),
        edge_source,
        edge_target,
    )
    vertex_out, vertex_state_out, context_out, context_state_out = pl.pallas_call(
        store_kernel,
        out_shape=tuple(jax.ShapeDtypeStruct(shape, F32) for shape in shapes),
        in_specs=[near] * 4,
        out_specs=(far,) * 4,
        scratch_shapes=[pltpu.SemaphoreType.DMA((6,))],
        compiler_params=pltpu.CompilerParams(vmem_limit_bytes=4 * 1024 * 1024),
    )(*results)
    return (
        vertex_out,
        vertex_state_out.reshape(row_count),
        context_out.reshape(block_rows, width),
        context_state_out.reshape(block_rows),
    )


def solution(mesh):
    matrix = P(("outer", "inner"), None)
    vector = P(("outer", "inner"))
    return jax.shard_map(
        functools.partial(body, mesh.shape["outer"], mesh.shape["inner"]),
        mesh=mesh,
        in_specs=(matrix, vector, matrix, vector, matrix, matrix),
        out_specs=(matrix, vector, matrix, vector),
        check_vma=False,
    )
```

```python
import functools

import jax
import jax.numpy as jnp
from jax import lax
from jax.experimental import pallas as pl
from jax.experimental.pallas import tpu as pltpu
from jax.sharding import PartitionSpec as P

ROUNDS = 3
CHUNK = 32
DEPTH = 4

MESH = pl.DeviceIdType.MESH
BF16 = jnp.bfloat16
F32 = jnp.float32


def kernel(
    n_outer,
    n_inner,
    vertex,
    vertex_state_in,
    context,
    context_state_in,
    edge_source_in,
    edge_target_in,
    rows,
    vertex_state_out,
    context_out,
    context_state_out,
    vertex_state,
    context_state,
    edge_source,
    edge_target,
    rows_b,
    rows_t,
    row_state,
    block,
    state,
    block_b,
    grads,
    counts,
    load_sem,
    send_sem,
    recv_sem,
    state_send_sem,
    state_recv_sem,
):
    pieces, chunk, width = context.shape
    row_count = rows.shape[0]
    block_rows = pieces * chunk
    edges = edge_source_in.shape[1] // ROUNDS
    hops = (ROUNDS - 1) * pieces

    i = lax.axis_index("inner")
    o = lax.axis_index("outer")
    right = {"inner": lax.rem(i + 1, n_inner)}
    left = {"inner": lax.rem(i + n_inner - 1, n_inner)}
    ahead = {"outer": lax.rem(o + 1, n_outer)}
    behind = {"outer": lax.rem(o + n_outer - 1, n_outer)}

    small_loads = [
        pltpu.make_async_copy(source, target, load_sem.at[3 + n])
        for n, (source, target) in enumerate(
            (
                (edge_source_in, edge_source),
                (edge_target_in, edge_target),
                (vertex_state_in, vertex_state),
                (context_state_in, context_state),
            )
        )
    ]
    for load in small_loads:
        load.start()
    halves = [pl.ds(0, row_count // 2), pl.ds(row_count // 2, row_count // 2)]
    load_rows = [
        pltpu.make_async_copy(vertex.at[half], rows.at[half], load_sem.at[7 * n])
        for n, half in enumerate(halves)
    ]
    load_first = pltpu.make_async_copy(context.at[0], block.at[0], load_sem.at[1])
    load_rest = pltpu.make_async_copy(
        context.at[pl.ds(1, pieces - 1)], block.at[pl.ds(1, pieces - 1)], load_sem.at[2]
    )
    for load in load_rows:
        load.start()
    load_first.start()
    load_rest.start()

    barrier = pltpu.get_barrier_semaphore()
    for neighbour in (left, right, behind, ahead):
        pl.semaphore_signal(barrier, inc=1, device_id=neighbour, device_id_type=MESH)

    def hop(s):
        return pltpu.make_async_remote_copy(
            src_ref=block.at[s],
            dst_ref=block.at[s + pieces],
            send_sem=send_sem.at[s],
            recv_sem=recv_sem.at[s + pieces],
            device_id=right,
            device_id_type=MESH,
        )

    def half_hop(h):
        span = pl.ds(h * (chunk // 2), chunk // 2)
        return pltpu.make_async_remote_copy(
            src_ref=block.at[hops - 1, span],
            dst_ref=block.at[hops - 1 + pieces, span],
            send_sem=send_sem.at[hops - 1 if h == 0 else hops + pieces],
            recv_sem=recv_sem.at[hops - 1 + pieces if h == 0 else hops + 2 * pieces],
            device_id=right,
            device_id_type=MESH,
        )

    def half_leave(h):
        span = pl.ds(h * (chunk // 2), chunk // 2)
        return pltpu.make_async_remote_copy(
            src_ref=block.at[hops - 1 + pieces, span],
            dst_ref=context_out.at[pieces - 1, span],
            send_sem=send_sem.at[hops + pieces - 1 + 2 * h],
            recv_sem=recv_sem.at[hops + 2 * pieces - 1 + 2 * h],
            device_id=ahead,
            device_id_type=MESH,
        )

    def state_move(r):
        return pltpu.make_async_remote_copy(
            src_ref=state.at[r],
            dst_ref=state.at[r + 1],
            send_sem=state_send_sem.at[r],
            recv_sem=state_recv_sem.at[r],
            device_id=ahead if r == ROUNDS - 1 else right,
            device_id_type=MESH,
        )

    def leave(k):
        return pltpu.make_async_remote_copy(
            src_ref=block.at[hops + k],
            dst_ref=context_out.at[k],
            send_sem=send_sem.at[hops + k],
            recv_sem=recv_sem.at[hops + pieces + k],
            device_id=ahead,
            device_id_type=MESH,
        )

    def count(r, first, number):
        span = pl.ds(r * edges, edges)
        target_hot = (
            edge_target[:, span]
            == lax.broadcasted_iota(jnp.int32, (number * chunk, edges), 0) + first * chunk
        ).astype(F32).astype(BF16)
        source_hot = (
            edge_source[:, span] == lax.broadcasted_iota(jnp.int32, (row_count, edges), 0)
        ).astype(F32).astype(BF16)
        counts[r, pl.ds(first, number)] = lax.dot_general(
            target_hot, source_hot, (((1,), (1,)), ((), ())), preferred_element_type=F32
        ).reshape(number, chunk, row_count)

    def update_chunk(slot, r, k, at=0, size=chunk):
        span = pl.ds(at, size)
        held = block[slot, span]
        held_b = held.astype(BF16)
        block_b[k, span] = held_b
        scores = lax.dot_general(
            held_b, rows_t[...], (((1,), (0,)), ((), ())), preferred_element_type=F32
        )
        prob = 1.0 / (1.0 + jnp.exp(-scores))
        grad = (prob * (1.0 / block_rows) - counts[r, k, span] * (1.0 - prob)).astype(BF16)
        grads[k, span] = grad
        chunk_grad = jnp.dot(grad, rows_b[...], preferred_element_type=F32)
        place = lax.broadcasted_iota(jnp.int32, (size, block_rows), 0) + (k * chunk + at)
        lane = lax.broadcasted_iota(jnp.int32, (size, block_rows), 1)
        mine = place == lane
        added = jnp.sum(chunk_grad * chunk_grad, axis=1, keepdims=True) * (1.0 / width)
        total = jnp.sum(jnp.where(mine, state[r], 0.0), axis=1, keepdims=True) + added
        block[slot, span] = held - chunk_grad * (0.1 * lax.rsqrt(total))
        state[r] += jnp.sum(jnp.where(mine, added, 0.0), axis=0, keepdims=True)

    def round_rows(half):
        rounded = rows[half].astype(BF16)
        rows_b[half] = rounded
        rows_t[:, half] = rounded.T

    def update_rows(last):
        for half in halves:
            rows_grad = lax.dot_general(
                grads[:, :, half].reshape(block_rows, row_count // 2),
                block_b[...].reshape(block_rows, width),
                (((0,), (0,)), ((), ())),
                preferred_element_type=F32,
            )
            total = row_state[half] + jnp.sum(rows_grad * rows_grad, axis=1, keepdims=True) * (
                1.0 / width
            )
            row_state[half] = total
            rows[half] = rows[half] - rows_grad * (0.1 * lax.rsqrt(total))
            if not last:
                round_rows(half)

    for load in small_loads:
        load.wait()
    state[0] = context_state[...]
    count(0, 0, 1)
    for half, load in zip(halves, load_rows):
        load.wait()
        round_rows(half)
    load_first.wait()
    update_chunk(0, 0, 0)
    pl.semaphore_wait(barrier, 4)
    hop(0).start()
    count(0, 1, pieces - 1)
    eye = lax.broadcasted_iota(jnp.int32, (row_count, row_count), 0) == lax.broadcasted_iota(
        jnp.int32, (row_count, row_count), 1
    )
    row_state[...] = jnp.sum(jnp.where(eye, vertex_state[...], 0.0), axis=1, keepdims=True)
    load_rest.wait()

    @pl.loop(1, pieces)
    def _(k):
        update_chunk(k, 0, k)

        @pl.when(k < DEPTH)
        def _():
            hop(k).start()

    state_move(0).start()
    for r in range(1, ROUNDS):
        count(r, 0, pieces)
    update_rows(False)

    for r in range(1, ROUNDS):

        last = r == ROUNDS - 1

        @pl.loop(0, pieces - 1 if last else pieces)
        def _(k):
            s = (r - 1) * pieces + k
            hop(s).wait_send()

            @pl.when(s + DEPTH < hops - 1)
            def _():
                hop(s + DEPTH).start()

            @pl.when(s + DEPTH == hops - 1)
            def _():
                half_hop(0).start()
                half_hop(1).start()

            hop(s).wait_recv()

            @pl.when(k == 0)
            def _():
                state_move(r - 1).wait_recv()

            update_chunk(s + pieces, r, k)
            if last:
                leave(k).start()

        if last:
            for h in range(2):
                half_hop(h).wait()
                update_chunk(hops - 1 + pieces, r, pieces - 1, h * (chunk // 2), chunk // 2)
                half_leave(h).start()
        state_move(r).start()
        update_rows(last)

    vertex_state_out[...] = jnp.sum(jnp.where(eye, row_state[...], 0.0), axis=0, keepdims=True)

    @pl.loop(0, pieces - 1)
    def _(k):
        leave(k).wait()

    for h in range(2):
        half_leave(h).wait()

    for r in range(ROUNDS):
        state_move(r).wait_send()
    state_move(ROUNDS - 1).wait_recv()
    context_state_out[...] = state[ROUNDS]


def store_kernel(*refs):
    sources, targets, sems = refs[:4], refs[4:8], refs[8]
    pairs = []
    for source, target in zip(sources, targets):
        lead = source.shape[0]
        parts = 1 if lead == 1 else 2
        for part in range(parts):
            span = pl.ds(part * (lead // parts), lead // parts)
            pairs.append((source.at[span], target.at[span]))
    copies = [
        pltpu.make_async_copy(source, target, sems.at[n])
        for n, (source, target) in enumerate(pairs)
    ]
    for copy in copies:
        copy.start()
    for copy in copies:
        copy.wait()


def body(n_outer, n_inner, vertex, vertex_state, context, context_state, edge_source, edge_target):
    row_count, width = vertex.shape
    block_rows = context.shape[0]
    pieces = block_rows // CHUNK
    slots = ROUNDS * pieces
    far = pl.BlockSpec(memory_space=pltpu.HBM)
    near = pl.BlockSpec(memory_space=pltpu.VMEM)
    shapes = (
        (row_count, width),
        (1, row_count),
        (pieces, CHUNK, width),
        (1, block_rows),
    )
    results = pl.pallas_call(
        functools.partial(kernel, n_outer, n_inner),
        out_shape=tuple(pltpu.VMEM(shape, F32) for shape in shapes),
        in_specs=[far] * 6,
        out_specs=(near,) * 4,
        scratch_shapes=[
            pltpu.VMEM((1, row_count), F32),
            pltpu.VMEM((1, block_rows), F32),
            pltpu.VMEM(edge_source.shape, jnp.int32),
            pltpu.VMEM(edge_target.shape, jnp.int32),
            pltpu.VMEM((row_count, width), BF16),
            pltpu.VMEM((width, row_count), BF16),
            pltpu.VMEM((row_count, 1), F32),
            pltpu.VMEM((slots, CHUNK, width), F32),
            pltpu.VMEM((ROUNDS + 1, 1, block_rows), F32),
            pltpu.VMEM((pieces, CHUNK, width), BF16),
            pltpu.VMEM((pieces, CHUNK, row_count), BF16),
            pltpu.VMEM((ROUNDS, pieces, CHUNK, row_count), F32),
            pltpu.SemaphoreType.DMA((8,)),
            pltpu.SemaphoreType.DMA((slots + 2,)),
            pltpu.SemaphoreType.DMA((slots + pieces + 2,)),
            pltpu.SemaphoreType.DMA((ROUNDS,)),
            pltpu.SemaphoreType.DMA((ROUNDS,)),
        ],
        compiler_params=pltpu.CompilerParams(
            collective_id=0, has_side_effects=True, vmem_limit_bytes=56 * 1024 * 1024
        ),
        cost_estimate=pl.CostEstimate(
            flops=ROUNDS * 2 * row_count * block_rows * (3 * width + 512),
            bytes_accessed=16 * row_count * width,
            transcendentals=ROUNDS * row_count * block_rows,
        ),
    )(
        vertex,
        vertex_state.reshape(1, row_count),
        context.reshape(pieces, CHUNK, width),
        context_state.reshape(1, block_rows),
        edge_source,
        edge_target,
    )
    vertex_out, vertex_state_out, context_out, context_state_out = pl.pallas_call(
        store_kernel,
        out_shape=tuple(jax.ShapeDtypeStruct(shape, F32) for shape in shapes),
        in_specs=[near] * 4,
        out_specs=(far,) * 4,
        scratch_shapes=[pltpu.SemaphoreType.DMA((6,))],
        compiler_params=pltpu.CompilerParams(vmem_limit_bytes=4 * 1024 * 1024),
    )(*results)
    return (
        vertex_out,
        vertex_state_out.reshape(row_count),
        context_out.reshape(block_rows, width),
        context_state_out.reshape(block_rows),
    )


def solution(mesh):
    matrix = P(("outer", "inner"), None)
    vector = P(("outer", "inner"))
    return jax.shard_map(
        functools.partial(body, mesh.shape["outer"], mesh.shape["inner"]),
        mesh=mesh,
        in_specs=(matrix, vector, matrix, vector, matrix, matrix),
        out_specs=(matrix, vector, matrix, vector),
        check_vma=False,
    )
```
